128 devices in a mesh: dp: 16 (over y_hi, z, core), fsdp: 8 (over x, y_lo).
Axes of the slice: x: 4, y: 4 (y_hi: 2, y_lo: 2; y = y_hi * 2 + y_lo), z: 4, core: 2. Of those that a mesh axis runs over, the one named last changes fastest.
Arguments:
- activations: bfloat16 [1, 16384, 8192], P(None, 'dp', 'fsdp'), may hold values from -6 to 6
- out_grads: bfloat16 [1, 16384, 22016], P(None, 'dp', 'fsdp'), may hold values from -2 to 2
- projector: bfloat16 [1, 8192, 1024], P(None, 'fsdp'), may hold values from -0.046875 to 0.046875
- first_moment: float32 [1, 22016, 1024], P(None, ('fsdp', 'dp')), may hold values from -16 to 16
- second_moment: float32 [1, 22016, 1024], P(None, ('fsdp', 'dp')), may hold values from 0.05 to 2
Outputs:
- weight_update: float32 [1, 8, 2752, 8192], P(None, None, 'dp', 'fsdp')
- first_new: float32 [1, 22016, 1024], P(None, ('fsdp', 'dp'))
- second_new: float32 [1, 22016, 1024], P(None, ('fsdp', 'dp'))
The draws below stay inside these ranges and needn't reach their ends.
All inputs are finite; a program needn't handle non-finite values.
Results may differ from the reference program's by a relative error of at most 0.018.
Values may be sent and summed in bfloat16 or wider, within the bound.
A program may use at most 64 MiB of HBM per device.

```python
import math
import jax
import jax.numpy as jnp
from jax import lax

D = 8192
FF = 22016
RANK = 1024
LAYERS = 1
TOK_DEV = 1024
TOKENS = 16384
N_DP = 16
N_FSDP = 8


def with_spikes(entries, rng, source, target, shards_of, factor):
    def block_of(axis_at):
        return (jnp.arange(entries.shape[axis_at]) // (entries.shape[axis_at] // shards_of)).reshape((-1,) + (1,) * (entries.ndim - 1 - axis_at))

    one_side = jax.random.permutation(rng, shards_of)[block_of(target)]
    other_side = (block_of(target) + shards_of // 2) % shards_of
    return jnp.where((block_of(source) == one_side) | (block_of(source) == other_side), factor * entries, entries)


def levels(own_key, dims, split, smallest, high):
    loudness, own = 1.0, jax.random.fold_in(own_key, 6)
    for position, shards_of in split:
        heights = jnp.exp(jax.random.uniform(jax.random.fold_in(own, position), (shards_of,), jnp.float32, smallest / len(split), high / len(split)))
        loudness = loudness * jnp.repeat(heights, dims[position] // shards_of).reshape([-1 if axis == position else 1 for axis in range(len(dims))])
    return loudness


def centred(key, dims, spread, limit, pieces=(), kind=jnp.bfloat16):
    entries = jax.random.normal(key, dims, jnp.float32) * spread
    if len(pieces) > 0:
        entries = levels(key, dims, pieces, -0.22, 0.18) * entries
    return jnp.clip(entries, min=-limit, max=limit).astype(kind)


def bell_draw_with(own_key, shape, deviation, most, cuts, heavy, held_as=jnp.bfloat16):
    values = deviation * jax.random.normal(own_key, shape, jnp.float32)
    if cuts:
        values = values * levels(own_key, shape, cuts, -0.22, 0.18)
    return jnp.clip(with_spikes(values, jax.random.fold_in(own_key, 3), *heavy), -most, most).astype(held_as)


def setup_inputs(seed: int = 0) -> dict:
    splits = jax.random.split(jax.random.key(seed), 6)
    return {
        "activations": centred(splits[0], (LAYERS, TOKENS, D), 1.0, 6.0, ((1, 16), (2, 8))),
        "out_grads": bell_draw_with(splits[1], (LAYERS, TOKENS, FF), (14.0 * TOKENS ** -0.5), 2.0, ((1, 16), (2, 8)), (1, 2, 16, 2.0)),
        "projector": centred(splits[2], (LAYERS, D, RANK), (16 * RANK) ** -0.5, 0.046875, ((1, 8),)),
        "first_moment": centred(splits[3], (LAYERS, FF, RANK), 3.0, 16.0, ((1, 128),), jnp.float32),
        "second_moment": jnp.clip(jnp.exp(math.log(2.0) - 3.6888794 * jax.random.uniform(splits[4], (LAYERS, FF, RANK), jnp.float32) ** levels(splits[4], (LAYERS, FF, RANK), ((1, 128),), -0.2, 0.2)), 0.05, 2.0),
    }


beta_first = 0.9
beta_second = 0.999
adam_count = 100.0
epsilon = 1e-08

def low_rank_gradient(projected, grads):
    blocks_proj = projected.reshape(N_DP, TOK_DEV, RANK)
    blocks_grad = grads.reshape(N_DP, TOK_DEV, FF)

    def accumulate(total, pair):
        term = jnp.dot(pair[1].T, pair[0], preferred_element_type=jnp.float32)
        rounded = lax.optimization_barrier(term.astype(jnp.bfloat16))
        return (total + rounded.astype(jnp.float32), None)
    total, unused = lax.scan(accumulate, jnp.zeros((FF, RANK), jnp.float32), (blocks_proj, blocks_grad))
    return total

def adam_direction(grad_low, first, second):
    first_next = beta_first * first + (1.0 - beta_first) * grad_low
    second_next = beta_second * second + (1.0 - beta_second) * grad_low * grad_low
    bias_first = 1.0 - beta_first ** adam_count
    bias_second = 1.0 - beta_second ** adam_count
    direction = first_next / bias_first / (jnp.sqrt(second_next / bias_second) + epsilon)
    return (first_next, second_next, direction.astype(jnp.bfloat16))

def reference(activations, out_grads, projector, first_moment, second_moment):
    updates = []
    firsts = []
    seconds = []
    for layer_index in range(LAYERS):
        projected = jnp.dot(activations[layer_index], projector[layer_index], preferred_element_type=jnp.float32).astype(jnp.bfloat16)
        grad_low = low_rank_gradient(projected, out_grads[layer_index])
        first_next, second_next, direction = adam_direction(grad_low, first_moment[layer_index], second_moment[layer_index])
        update = jnp.dot(direction, projector[layer_index].T, preferred_element_type=jnp.float32)
        updates.append(update.reshape(N_FSDP, FF // N_FSDP, D))
        firsts.append(first_next)
        seconds.append(second_next)
    return (jnp.stack(updates), jnp.stack(firsts), jnp.stack(seconds))
```

```python
import functools

import jax
import jax.numpy as jnp
from jax import lax
from jax.experimental import pallas as pl
from jax.experimental.pallas import tpu as pltpu
from jax.sharding import PartitionSpec as P

MESH = pl.DeviceIdType.MESH
F32, BF16 = jnp.float32, jnp.bfloat16

beta_first = 0.9
beta_second = 0.999
adam_count = 100.0
epsilon = 1e-08

CHUNKS = 4
RS_X_FIRST = (True, False, True, False)
AG_X_FIRST = (False, True, False, True)
DIR_X_FIRST = (True, False, True, False)
STAGE_AT = (0, 6, 9, 11, 16, 20, 28, 31, 34, 39)
CHUNK_EVERY = 9.0


def adam_direction(grad_low, first, second):
    first_next = beta_first * first + (1.0 - beta_first) * grad_low
    second_next = beta_second * second + (1.0 - beta_second) * grad_low * grad_low
    bias_first = 1.0 - beta_first**adam_count
    bias_second = 1.0 - beta_second**adam_count
    direction = first_next / bias_first / (jnp.sqrt(second_next / bias_second) + epsilon)
    return (first_next, second_next, direction.astype(BF16))


def strips(rows, step, body):
    def one(index, carry):
        body(pl.ds(pl.multiple_of(index * step, step), step))
        return carry

    lax.fori_loop(0, rows // step, one, 0)


def wide(ref, *index):
    return ref[index].astype(F32)


def exchange_kernel(
    act_hbm, grads_hbm, basis_hbm, first_hbm, second_hbm,
    dirs_hbm, first_out, second_out,
    act, basis, grads_t, first, second, product,
    part, rs_a, rs_s, rs_b, projected,
    terms, core_in, z_out, z_in, y_out, y_in, dirs,
    load_sem, store_sem, send_sem, recv_sem,
):
    dp, fs = lax.axis_index("dp"), lax.axis_index("fsdp")
    yh, z, core = dp // 8, (dp // 2) % 4, dp % 2
    x, yl = fs // 2, fs % 2
    chunk = basis.shape[1] // CHUNKS
    row_tiles = basis.shape[1] // 128
    owned = first.shape[0] // row_tiles
    padded = dirs.shape[3]
    tokens = part.shape[3]
    features = act.shape[0]

    def along_x(d):
        return (dp, ((x + d) % 4) * 2 + yl)

    def along_z(d):
        return (yh * 8 + ((z + d) % 4) * 2 + core, fs)

    y_near = (dp, x * 2 + 1 - yl)
    y_far = ((1 - yh) * 8 + z * 2 + core, fs)
    sibling = (yh * 8 + z * 2 + 1 - core, fs)

    loads = [
        pltpu.make_async_copy(act_hbm.at[0], act, load_sem.at[0]),
        pltpu.make_async_copy(basis_hbm.at[0], basis, load_sem.at[1]),
        pltpu.make_async_copy(grads_hbm.at[0], grads_t, load_sem.at[2]),
        pltpu.make_async_copy(first_hbm, first, load_sem.at[3]),
        pltpu.make_async_copy(second_hbm, second, load_sem.at[4]),
    ]
    for load in loads:
        load.start()

    barrier = pltpu.get_barrier_semaphore()
    peers = [along_x(1), along_x(2), along_x(3), along_z(1), along_z(2), along_z(3), y_near, y_far, sibling]
    for peer in peers:
        pl.semaphore_signal(barrier, inc=1, device_id=peer, device_id_type=MESH)

    sent = []

    def remote(source, target, c, slot, peer):
        return pltpu.make_async_remote_copy(
            src_ref=source, dst_ref=target, send_sem=send_sem.at[c, slot], recv_sem=recv_sem.at[c, slot],
            device_id=peer, device_id_type=MESH,
        )

    def send(source, target, c, slot, peer):
        copy = remote(source, target, c, slot, peer)
        copy.start()
        sent.append(copy)

    def arrived(target, c, slot, peer):
        remote(target, target, c, slot, peer).wait_recv()


    def project(c):
        columns = slice(c * chunk, (c + 1) * chunk)
        half = features // 2

        def one(index, carry):
            rows = pl.ds(pl.multiple_of(index * half, half), half)
            value = jnp.dot(act[rows, :], basis[:, columns], preferred_element_type=F32)
            part[c, index] = value.astype(BF16).reshape(4, tokens, chunk)
            return carry

        lax.fori_loop(0, 2, one, 0)

    def reduce_first(c):
        if RS_X_FIRST[c]:
            for d in (2, 1, 3):
                send(part.at[c, :, (x + d) % 4], rs_a.at[c, pl.ds((d - 1) * 2, 2)], c, d - 1, along_x(d))
        else:
            send(part.at[c, 1 - yl], rs_a.at[c, pl.ds(0, 4)], c, 3, y_near)

    def reduce_second(c):
        if RS_X_FIRST[c]:
            for d in (1, 3, 2):
                arrived(rs_a.at[c, pl.ds((d - 1) * 2, 2)], c, d - 1, along_x(d))
            other = 1 - yl

            def body(rows):
                total = wide(part, c, other, x, rows)
                for d in range(3):
                    total += wide(rs_a, c, 2 * d + other, rows)
                rs_s[c, 0, rows] = total.astype(BF16)

            strips(tokens, 32, body)
            send(rs_s.at[c, 0], rs_b.at[c, 0], c, 3, y_near)
        else:
            arrived(rs_a.at[c, pl.ds(0, 4)], c, 3, y_near)
            for d in (2, 1, 3):
                to = (x + d) % 4

                def body(rows):
                    total = wide(part, c, yl, to, rows) + wide(rs_a, c, to, rows)
                    rs_s[c, d - 1, rows] = total.astype(BF16)

                strips(tokens, 32, body)
                send(rs_s.at[c, d - 1], rs_b.at[c, d - 1], c, d - 1, along_x(d))

    def reduce_last(c):
        if RS_X_FIRST[c]:
            arrived(rs_b.at[c, 0], c, 3, y_near)

            def body(rows):
                total = wide(part, c, yl, x, rows) + wide(rs_b, c, 0, rows)
                for d in range(3):
                    total += wide(rs_a, c, 2 * d + yl, rows)
                projected[c, yl, x, rows] = total.astype(BF16)

        else:
            for d in (1, 3, 2):
                arrived(rs_b.at[c, d - 1], c, d - 1, along_x(d))

            def body(rows):
                total = wide(part, c, yl, x, rows) + wide(rs_a, c, x, rows)
                for d in range(3):
                    total += wide(rs_b, c, d, rows)
                projected[c, yl, x, rows] = total.astype(BF16)

        strips(tokens, 32, body)

    def gather_first(buffer, c, slot, x_first):
        mine = buffer.at[c, yl, x]
        if x_first:
            for d in (2, 1, 3):
                send(mine, mine, c, slot + d - 1, along_x(d))
        else:
            send(mine, mine, c, slot + 3, y_near)

    def gather_second(buffer, c, slot, x_first):
        if x_first:
            for d in (1, 3, 2):
                arrived(buffer.at[c, yl, (x + 4 - d) % 4], c, slot + d - 1, along_x(d))
            send(buffer.at[c, yl], buffer.at[c, yl], c, slot + 3, y_near)
        else:
            arrived(buffer.at[c, 1 - yl, x], c, slot + 3, y_near)
            for d in (2, 1, 3):
                send(buffer.at[c, :, x], buffer.at[c, :, x], c, slot + d - 1, along_x(d))

    def gather_last(buffer, c, slot, x_first):
        if x_first:
            arrived(buffer.at[c, 1 - yl], c, slot + 3, y_near)
        else:
            for d in (1, 3, 2):
                arrived(buffer.at[c, :, (x + 4 - d) % 4], c, slot + d - 1, along_x(d))

    def gradient(c):
        rows_all = grads_t.shape[0]
        tile = rows_all // 4

        def one(index, carry):
            rows = pl.ds(pl.multiple_of(index * tile, tile), tile)
            value = jnp.dot(
                grads_t[rows, :], projected[c].reshape(features, chunk), preferred_element_type=F32
            )
            product[rows, :] = value
            return carry

        lax.fori_loop(0, 4, one, 0)

        def two(pair, carry):
            for which in range(2):
                shift = which * owned % 8
                start = pl.multiple_of(pair * (2 * owned) + which * owned - shift, 8)
                value = product[pl.ds(start, padded + 8), :]
                terms[c, which, pair // 4, pair % 4] = value[shift : shift + padded].astype(BF16)
            return carry

        lax.fori_loop(0, 8, two, 0)
        send(terms.at[c, 1 - core], core_in.at[c], c, 8, sibling)

    def core_sum(c):
        arrived(core_in.at[c], c, 8, sibling)
        for d in (2, 1, 3):
            to = (z + d) % 4
            for h in range(2):

                def body(rows):
                    total = wide(terms, c, core, h, to, rows) + wide(core_in, c, h, to, rows)
                    z_out[c, d - 1, h, rows] = total.astype(BF16)

                strips(padded, 16, body)
            send(z_out.at[c, d - 1], z_in.at[c, d - 1], c, 8 + d, along_z(d))

    def z_sum(c, h, rows):
        total = wide(terms, c, core, h, z, rows) + wide(core_in, c, h, z, rows)
        for d in range(3):
            total += wide(z_in, c, d, h, rows)
        return total

    def z_stage(c):
        for d in (1, 3, 2):
            arrived(z_in.at[c, d - 1], c, 8 + d, along_z(d))

        def body(rows):
            y_out[c, rows] = z_sum(c, 1 - yh, rows).astype(BF16)

        strips(padded, 16, body)
        send(y_out.at[c], y_in.at[c], c, 12, y_far)

    def adam(c):
        if c == 0:
            loads[3].wait()
            loads[4].wait()
        arrived(y_in.at[c], c, 12, y_far)

        def update(start, rows):
            low = z_sum(c, yh, pl.ds(start, rows)) + wide(y_in, c, pl.ds(start, rows))
            for part_of in range(chunk // 128):
                lanes = slice(part_of * 128, (part_of + 1) * 128)
                column = c * (chunk // 128) + part_of
                here = pl.ds(start * row_tiles + column, rows, stride=row_tiles)
                first_next, second_next, direction = adam_direction(low[:, lanes], first[here, :], second[here, :])
                first[here, :] = first_next
                second[here, :] = second_next
                dirs[c, yl, x, pl.ds(start, rows), lanes] = direction

        whole = owned // 16 * 16

        def one(index, carry):
            update(pl.multiple_of(index * 16, 16), 16)
            return carry

        lax.fori_loop(0, whole // 16, one, 0)
        if owned > whole:
            update(whole, owned - whole)

    def out_copies(c):
        columns = pl.ds(c * chunk, chunk)
        return [pltpu.make_async_copy(dirs.at[c], dirs_hbm.at[:, :, :, columns], store_sem.at[c])]

    barrier_done = []

    def stage(s, c):
        if s == 0:
            if c == 0:
                loads[0].wait()
                loads[1].wait()
            project(c)
            if not barrier_done:
                pl.semaphore_wait(barrier, len(peers))
                barrier_done.append(True)
            reduce_first(c)
        elif s == 1:
            reduce_second(c)
        elif s == 2:
            reduce_last(c)
            gather_first(projected, c, 4, AG_X_FIRST[c])
        elif s == 3:
            gather_second(projected, c, 4, AG_X_FIRST[c])
        elif s == 4:
            gather_last(projected, c, 4, AG_X_FIRST[c])
            if c == 0:
                loads[2].wait()
            gradient(c)
        elif s == 5:
            core_sum(c)
        elif s == 6:
            z_stage(c)
        elif s == 7:
            adam(c)
            gather_first(dirs, c, 13, DIR_X_FIRST[c])
        elif s == 8:
            gather_second(dirs, c, 13, DIR_X_FIRST[c])
        else:
            gather_last(dirs, c, 13, DIR_X_FIRST[c])
            for copy in out_copies(c):
                copy.start()

    order = sorted(
        ((STAGE_AT[s] + (CHUNK_EVERY * c if s else 0.0), c, s) for c in range(CHUNKS) for s in range(len(STAGE_AT)))
    )
    moments = [
        pltpu.make_async_copy(first, first_out, store_sem.at[CHUNKS]),
        pltpu.make_async_copy(second, second_out, store_sem.at[CHUNKS + 1]),
    ]
    for _, c, s in order:
        stage(s, c)
        if s == 7 and c == CHUNKS - 1:
            for copy in moments:
                copy.start()
    for copy in sent:
        copy.wait_send()
    for c in range(CHUNKS):
        for copy in out_copies(c):
            copy.wait()
    for copy in moments:
        copy.wait()


def exchange(activations, grads_t, projector, first, second, owned):
    features = activations.shape[1]
    width = grads_t.shape[1]
    depth, rank = projector.shape[1:]
    padded = -(-owned // 16) * 16
    chunk = rank // CHUNKS
    tokens = features // 8
    in_hbm = pl.BlockSpec(memory_space=pl.ANY)
    C = CHUNKS
    scratch = [
        pltpu.VMEM((features, depth), BF16),
        pltpu.VMEM((depth, rank), BF16),
        pltpu.VMEM((width, features), BF16),
        pltpu.VMEM(first.shape, F32),
        pltpu.VMEM(first.shape, F32),
        pltpu.VMEM((width + 16, chunk), F32),
        pltpu.VMEM((C, 2, 4, tokens, chunk), BF16),
        pltpu.VMEM((C, 6, tokens, chunk), BF16),
        pltpu.VMEM((C, 3, tokens, chunk), BF16),
        pltpu.VMEM((C, 3, tokens, chunk), BF16),
        pltpu.VMEM((C, 2, 4, tokens, chunk), BF16),
        pltpu.VMEM((C, 2, 2, 4, padded, chunk), BF16),
        pltpu.VMEM((C, 2, 4, padded, chunk), BF16),
        pltpu.VMEM((C, 3, 2, padded, chunk), BF16),
        pltpu.VMEM((C, 3, 2, padded, chunk), BF16),
        pltpu.VMEM((C, padded, chunk), BF16),
        pltpu.VMEM((C, padded, chunk), BF16),
        pltpu.VMEM((C, 2, 4, padded, chunk), BF16),
        pltpu.SemaphoreType.DMA((5,)),
        pltpu.SemaphoreType.DMA((C + 2,)),
        pltpu.SemaphoreType.DMA((C, 17)),
        pltpu.SemaphoreType.DMA((C, 17)),
    ]
    return pl.pallas_call(
        exchange_kernel,
        out_shape=(
            jax.ShapeDtypeStruct((2, 4, padded, rank), BF16),
            jax.ShapeDtypeStruct(first.shape, F32),
            jax.ShapeDtypeStruct(first.shape, F32),
        ),
        in_specs=[in_hbm] * 5,
        out_specs=(in_hbm,) * 3,
        scratch_shapes=scratch,
        compiler_params=pltpu.CompilerParams(
            collective_id=0, has_side_effects=True, vmem_limit_bytes=60 << 20
        ),
        name="exchange",
    )(activations, grads_t, projector, first, second)


def expand_kernel(
    dirs_hbm, basis, first_in, second_in, update_out, first_out, second_out, dirs, update, load_sem, store_sem, sem
):
    load = pltpu.make_async_copy(dirs_hbm, dirs, load_sem)
    load.start()
    moments = [
        pltpu.make_async_copy(first_in, first_out, sem.at[0]),
        pltpu.make_async_copy(second_in, second_out, sem.at[1]),
    ]
    for copy in moments:
        copy.start()
    padded, rank = dirs.shape[2:]
    owned = update.shape[1] // 8
    depth = basis.shape[1]
    load.wait()

    def store(column):
        return pltpu.make_async_copy(
            update.at[column], update_out.at[:, pl.ds(pl.multiple_of(column * 128, 128), 128)], store_sem.at[column]
        )

    def tile(index, carry):
        rows = pl.ds(pl.multiple_of(index * 256, 256), 256)
        total = lax.dot_general(
            dirs[...].reshape(8 * padded, rank), basis[0, rows, :],
            (((1,), (1,)), ((), ())), preferred_element_type=F32,
        )
        for half in range(2):
            for yl in range(2):
                for x in range(4):
                    start = (yl * 4 + x) * padded
                    update[index * 2 + half, pl.ds(x * 2 + yl, owned, stride=8), :] = total[
                        start : start + owned, half * 128 : (half + 1) * 128
                    ]
            store(index * 2 + half).start()
        return carry

    lax.fori_loop(0, depth // 256, tile, 0)
    for column in range(depth // 128):
        store(column).wait()
    for copy in moments:
        copy.wait()


def expand(dirs, projector, first, second, owned):
    depth, rank = projector.shape[1:]
    in_hbm = pl.BlockSpec(memory_space=pl.ANY)
    moment = jax.ShapeDtypeStruct(first.shape, F32)
    return pl.pallas_call(
        expand_kernel,
        out_shape=(jax.ShapeDtypeStruct((owned * 8, depth), F32), moment, moment),
        in_specs=[in_hbm, pl.BlockSpec(memory_space=pltpu.VMEM), in_hbm, in_hbm],
        out_specs=(in_hbm,) * 3,
        scratch_shapes=[
            pltpu.VMEM(dirs.shape, BF16),
            pltpu.VMEM((depth // 128, owned * 8, 128), F32),
            pltpu.SemaphoreType.DMA,
            pltpu.SemaphoreType.DMA((depth // 128,)),
            pltpu.SemaphoreType.DMA((2,)),
        ],
        compiler_params=pltpu.CompilerParams(vmem_limit_bytes=48 << 20),
        name="expand",
    )(dirs, projector, first, second)


def local(activations, out_grads, projector, first_moment, second_moment):
    owned, rank = first_moment.shape[1:]
    flat = (owned * (rank // 128), 128)
    dirs, first, second = exchange(
        activations, jnp.swapaxes(out_grads, 1, 2), projector, first_moment.reshape(flat), second_moment.reshape(flat),
        owned,
    )
    update, first, second = expand(dirs, projector, first, second, owned)
    update = update.reshape(owned, 8, -1).transpose(1, 0, 2)[None]
    return update, first.reshape(first_moment.shape), second.reshape(second_moment.shape)


def solution(mesh):
    in_specs = (
        P(None, "dp", "fsdp"),
        P(None, "dp", "fsdp"),
        P(None, "fsdp", None),
        P(None, ("fsdp", "dp"), None),
        P(None, ("fsdp", "dp"), None),
    )
    out_specs = (
        P(None, None, "dp", "fsdp"),
        P(None, ("fsdp", "dp"), None),
        P(None, ("fsdp", "dp"), None),
    )
    return jax.shard_map(local, mesh=mesh, in_specs=in_specs, out_specs=out_specs, check_vma=False)
```

```python
import functools

import jax
import jax.numpy as jnp
from jax import lax
from jax.experimental import pallas as pl
from jax.experimental.pallas import tpu as pltpu
from jax.sharding import PartitionSpec as P

MESH = pl.DeviceIdType.MESH
F32, BF16 = jnp.float32, jnp.bfloat16

beta_first = 0.9
beta_second = 0.999
adam_count = 100.0
epsilon = 1e-08

CHUNKS = 8
RS_X_FIRST = (True, False, True, False, True, False, True, False)
AG_X_FIRST = (False, True, False, True, False, True, False, True)
DIR_X_FIRST = (True, False, True, False, True, False, True, False)
ORDER = (
    4, 7, 3, 0, 7, 4, 5, 2, 4, 3, 7, 0, 1, 4, 0, 3, 2, 1, 7, 0,
    6, 4, 3, 4, 2, 7, 5, 1, 7, 3, 2, 6, 0, 3, 4, 6, 1, 5, 0, 2,
    6, 7, 5, 2, 1, 4, 3, 0, 7, 1, 6, 3, 5, 4, 0, 6, 7, 5, 3, 1,
    2, 0, 7, 6, 5, 2, 1, 6, 5, 1, 2, 3, 5, 6, 1, 5, 4, 2, 0, 6,
)


def adam_direction(grad_low, first, second):
    first_next = beta_first * first + (1.0 - beta_first) * grad_low
    second_next = beta_second * second + (1.0 - beta_second) * grad_low * grad_low
    bias_first = 1.0 - beta_first**adam_count
    bias_second = 1.0 - beta_second**adam_count
    direction = first_next / bias_first / (jnp.sqrt(second_next / bias_second) + epsilon)
    return (first_next, second_next, direction.astype(BF16))


def wide(ref, *index):
    return ref[index].astype(F32)


def exchange_kernel(
    act_hbm, grads_hbm, basis_hbm, first_hbm, second_hbm,
    dirs_hbm, first_out, second_out,
    act, basis, grads_t, first, second, product,
    part, rs_a, rs_s, rs_b, projected,
    terms, core_in, z_out, z_in, y_out, y_in, dirs,
    load_sem, store_sem, send_sem, recv_sem,
):
    dp, fs = lax.axis_index("dp"), lax.axis_index("fsdp")
    yh, z, core = dp // 8, (dp // 2) % 4, dp % 2
    x, yl = fs // 2, fs % 2
    chunk = basis.shape[1] // CHUNKS
    row_tiles = basis.shape[1] // 128
    owned = first.shape[0] // row_tiles
    padded = dirs.shape[3]
    tokens = part.shape[3]
    features = act.shape[0]

    def along_x(d):
        return (dp, ((x + d) % 4) * 2 + yl)

    def along_z(d):
        return (yh * 8 + ((z + d) % 4) * 2 + core, fs)

    y_near = (dp, x * 2 + 1 - yl)
    y_far = ((1 - yh) * 8 + z * 2 + core, fs)
    sibling = (yh * 8 + z * 2 + 1 - core, fs)

    loads = [
        pltpu.make_async_copy(act_hbm.at[0], act, load_sem.at[0]),
        pltpu.make_async_copy(basis_hbm.at[0], basis, load_sem.at[1]),
        pltpu.make_async_copy(grads_hbm.at[0], grads_t, load_sem.at[2]),
        pltpu.make_async_copy(first_hbm, first, load_sem.at[3]),
        pltpu.make_async_copy(second_hbm, second, load_sem.at[4]),
    ]
    for load in loads:
        load.start()

    barrier = pltpu.get_barrier_semaphore()
    peers = [along_x(1), along_x(2), along_x(3), along_z(1), along_z(2), along_z(3), y_near, y_far, sibling]
    for peer in peers:
        pl.semaphore_signal(barrier, inc=1, device_id=peer, device_id_type=MESH)

    sent = []

    def remote(source, target, c, slot, peer):
        return pltpu.make_async_remote_copy(
            src_ref=source, dst_ref=target, send_sem=send_sem.at[c, slot], recv_sem=recv_sem.at[c, slot],
            device_id=peer, device_id_type=MESH,
        )

    def send(source, target, c, slot, peer):
        copy = remote(source, target, c, slot, peer)
        copy.start()
        sent.append(copy)

    def arrived(target, c, slot, peer):
        remote(target, target, c, slot, peer).wait_recv()


    def project(c):
        columns = slice(c * chunk, (c + 2) * chunk)
        half = features // 2

        def one(index, carry):
            rows = pl.ds(pl.multiple_of(index * half, half), half)
            value = jnp.dot(act[rows, :], basis[:, columns], preferred_element_type=F32)
            value = value.astype(BF16)
            for which in range(2):
                part[c + which, index] = value[:, which * chunk : (which + 1) * chunk].reshape(4, tokens, chunk)
            return carry

        lax.fori_loop(0, 2, one, 0)

    def reduce_first(c):
        if RS_X_FIRST[c]:
            for d in (2, 1, 3):
                send(part.at[c, :, (x + d) % 4], rs_a.at[c, pl.ds((d - 1) * 2, 2)], c, d - 1, along_x(d))
        else:
            send(part.at[c, 1 - yl], rs_a.at[c, pl.ds(0, 4)], c, 3, y_near)

    def reduce_second(c):
        if RS_X_FIRST[c]:
            for d in (1, 3, 2):
                arrived(rs_a.at[c, pl.ds((d - 1) * 2, 2)], c, d - 1, along_x(d))
            other = 1 - yl

            total = wide(part, c, other, x)
            for d in range(3):
                total += wide(rs_a, c, 2 * d + other)
            rs_s[c, 0] = total.astype(BF16)
            send(rs_s.at[c, 0], rs_b.at[c, 0], c, 3, y_near)
        else:
            arrived(rs_a.at[c, pl.ds(0, 4)], c, 3, y_near)
            for d in (2, 1, 3):
                to = (x + d) % 4
                rs_s[c, d - 1] = (wide(part, c, yl, to) + wide(rs_a, c, to)).astype(BF16)
                send(rs_s.at[c, d - 1], rs_b.at[c, d - 1], c, d - 1, along_x(d))

    def reduce_last(c):
        if RS_X_FIRST[c]:
            arrived(rs_b.at[c, 0], c, 3, y_near)
            total = wide(part, c, yl, x) + wide(rs_b, c, 0)
            for d in range(3):
                total += wide(rs_a, c, 2 * d + yl)
        else:
            for d in (1, 3, 2):
                arrived(rs_b.at[c, d - 1], c, d - 1, along_x(d))
            total = wide(part, c, yl, x) + wide(rs_a, c, x)
            for d in range(3):
                total += wide(rs_b, c, d)
        projected[c, yl, x] = total.astype(BF16)

    def gather_first(buffer, c, slot, x_first):
        mine = buffer.at[c, yl, x]
        if x_first:
            for d in (2, 1, 3):
                send(mine, mine, c, slot + d - 1, along_x(d))
        else:
            send(mine, mine, c, slot + 3, y_near)

    def gather_second(buffer, c, slot, x_first):
        if x_first:
            for d in (1, 3, 2):
                arrived(buffer.at[c, yl, (x + 4 - d) % 4], c, slot + d - 1, along_x(d))
            send(buffer.at[c, yl], buffer.at[c, yl], c, slot + 3, y_near)
        else:
            arrived(buffer.at[c, 1 - yl, x], c, slot + 3, y_near)
            for d in (2, 1, 3):
                send(buffer.at[c, :, x], buffer.at[c, :, x], c, slot + d - 1, along_x(d))

    def gather_last(buffer, c, slot, x_first):
        if x_first:
            arrived(buffer.at[c, 1 - yl], c, slot + 3, y_near)
        else:
            for d in (1, 3, 2):
                arrived(buffer.at[c, :, (x + 4 - d) % 4], c, slot + d - 1, along_x(d))

    def gradient(c):
        rows_all = grads_t.shape[0]
        tile = rows_all // 4

        def one(index, carry):
            rows = pl.ds(pl.multiple_of(index * tile, tile), tile)
            value = jnp.dot(
                grads_t[rows, :], projected[c].reshape(features, chunk), preferred_element_type=F32
            )
            product[rows, :] = value
            return carry

        lax.fori_loop(0, 4, one, 0)

        def two(pair, carry):
            for which in range(2):
                shift = which * owned % 8
                start = pl.multiple_of(pair * (2 * owned) + which * owned - shift, 8)
                value = product[pl.ds(start, padded + 8), :]
                terms[c, which, pair // 4, pair % 4] = value[shift : shift + padded].astype(BF16)
            return carry

        lax.fori_loop(0, 8, two, 0)
        send(terms.at[c, 1 - core], core_in.at[c], c, 8, sibling)

    def core_sum(c):
        arrived(core_in.at[c], c, 8, sibling)
        for d in (2, 1, 3):
            to = (z + d) % 4
            for h in range(2):
                z_out[c, d - 1, h] = (wide(terms, c, core, h, to) + wide(core_in, c, h, to)).astype(BF16)
            send(z_out.at[c, d - 1], z_in.at[c, d - 1], c, 8 + d, along_z(d))

    def z_sum(c, h):
        total = wide(terms, c, core, h, z) + wide(core_in, c, h, z)
        for d in range(3):
            total += wide(z_in, c, d, h)
        return total

    def z_stage(c):
        for d in (1, 3, 2):
            arrived(z_in.at[c, d - 1], c, 8 + d, along_z(d))
        y_out[c] = z_sum(c, 1 - yh).astype(BF16)
        send(y_out.at[c], y_in.at[c], c, 12, y_far)

    def adam(c):
        if 3 not in waited:
            loads[3].wait()
            loads[4].wait()
            waited.add(3)
        arrived(y_in.at[c], c, 12, y_far)

        low = (z_sum(c, yh) + wide(y_in, c))[:owned]
        for part_of in range(chunk // 128):
            lanes = slice(part_of * 128, (part_of + 1) * 128)
            here = pl.ds(c * (chunk // 128) + part_of, owned, stride=row_tiles)
            first_next, second_next, direction = adam_direction(low[:, lanes], first[here, :], second[here, :])
            first[here, :] = first_next
            second[here, :] = second_next
            dirs[c, yl, x, :owned, lanes] = direction

    def out_copies(c):
        columns = pl.ds(c * chunk, chunk)
        return [pltpu.make_async_copy(dirs.at[c], dirs_hbm.at[:, :, :, columns], store_sem.at[c])]

    barrier_done, projected_pairs, waited = [], set(), set()

    def stage(s, c):
        if s == 0:
            if not projected_pairs:
                loads[0].wait()
                loads[1].wait()
            if c // 2 not in projected_pairs:
                project(c // 2 * 2)
                projected_pairs.add(c // 2)
            if not barrier_done:
                pl.semaphore_wait(barrier, len(peers))
                barrier_done.append(True)
            reduce_first(c)
        elif s == 1:
            reduce_second(c)
        elif s == 2:
            reduce_last(c)
            gather_first(projected, c, 4, AG_X_FIRST[c])
        elif s == 3:
            gather_second(projected, c, 4, AG_X_FIRST[c])
        elif s == 4:
            gather_last(projected, c, 4, AG_X_FIRST[c])
            if 2 not in waited:
                loads[2].wait()
                waited.add(2)
            gradient(c)
        elif s == 5:
            core_sum(c)
        elif s == 6:
            z_stage(c)
        elif s == 7:
            adam(c)
            gather_first(dirs, c, 13, DIR_X_FIRST[c])
        elif s == 8:
            gather_second(dirs, c, 13, DIR_X_FIRST[c])
        else:
            gather_last(dirs, c, 13, DIR_X_FIRST[c])
            for copy in out_copies(c):
                copy.start()

    order, turns = [], [0] * CHUNKS
    for c in ORDER:
        order.append((None, c, turns[c]))
        turns[c] += 1
    moments = [
        pltpu.make_async_copy(first, first_out, store_sem.at[CHUNKS]),
        pltpu.make_async_copy(second, second_out, store_sem.at[CHUNKS + 1]),
    ]
    last_adam = [c for _, c, s in order if s == 7][-1]
    for _, c, s in order:
        stage(s, c)
        if s == 7 and c == last_adam:
            for copy in moments:
                copy.start()
    for copy in sent:
        copy.wait_send()
    for c in range(CHUNKS):
        for copy in out_copies(c):
            copy.wait()
    for copy in moments:
        copy.wait()


def exchange(activations, grads_t, projector, first, second, owned):
    features = activations.shape[1]
    width = grads_t.shape[1]
    depth, rank = projector.shape[1:]
    padded = -(-owned // 16) * 16
    chunk = rank // CHUNKS
    tokens = features // 8
    in_hbm = pl.BlockSpec(memory_space=pl.ANY)
    C = CHUNKS
    scratch = [
        pltpu.VMEM((features, depth), BF16),
        pltpu.VMEM((depth, rank), BF16),
        pltpu.VMEM((width, features), BF16),
        pltpu.VMEM(first.shape, F32),
        pltpu.VMEM(first.shape, F32),
        pltpu.VMEM((width + 16, chunk), F32),
        pltpu.VMEM((C, 2, 4, tokens, chunk), BF16),
        pltpu.VMEM((C, 6, tokens, chunk), BF16),
        pltpu.VMEM((C, 3, tokens, chunk), BF16),
        pltpu.VMEM((C, 3, tokens, chunk), BF16),
        pltpu.VMEM((C, 2, 4, tokens, chunk), BF16),
        pltpu.VMEM((C, 2, 2, 4, padded, chunk), BF16),
        pltpu.VMEM((C, 2, 4, padded, chunk), BF16),
        pltpu.VMEM((C, 3, 2, padded, chunk), BF16),
        pltpu.VMEM((C, 3, 2, padded, chunk), BF16),
        pltpu.VMEM((C, padded, chunk), BF16),
        pltpu.VMEM((C, padded, chunk), BF16),
        pltpu.VMEM((C, 2, 4, padded, chunk), BF16),
        pltpu.SemaphoreType.DMA((5,)),
        pltpu.SemaphoreType.DMA((C + 2,)),
        pltpu.SemaphoreType.DMA((C, 17)),
        pltpu.SemaphoreType.DMA((C, 17)),
    ]
    return pl.pallas_call(
        exchange_kernel,
        out_shape=(
            jax.ShapeDtypeStruct((2, 4, padded, rank), BF16),
            jax.ShapeDtypeStruct(first.shape, F32),
            jax.ShapeDtypeStruct(first.shape, F32),
        ),
        in_specs=[in_hbm] * 5,
        out_specs=(in_hbm,) * 3,
        scratch_shapes=scratch,
        compiler_params=pltpu.CompilerParams(
            collective_id=0, has_side_effects=True, vmem_limit_bytes=60 << 20
        ),
        name="exchange",
    )(activations, grads_t, projector, first, second)


EXPAND_ROWS = ((0, 64), (64, 64), (128, 48))


def expand_kernel(
    dirs_hbm, basis_hbm, first_in, second_in, update_out, first_out, second_out,
    dirs, basis, update, first, second, load_sem, store_sem, sem,
):
    basis_load = pltpu.make_async_copy(basis_hbm.at[0], basis, sem.at[0])
    basis_load.start()
    loads = [
        pltpu.make_async_copy(dirs_hbm.at[:, :, pl.ds(*rows)], dirs.at[:, :, pl.ds(*rows)], load_sem.at[group])
        for group, rows in enumerate(EXPAND_ROWS)
    ]
    for load in loads:
        load.start()
    moments_in = [
        pltpu.make_async_copy(first_in, first, sem.at[1]),
        pltpu.make_async_copy(second_in, second, sem.at[2]),
    ]
    moments_out = [
        pltpu.make_async_copy(first, first_out, sem.at[3]),
        pltpu.make_async_copy(second, second_out, sem.at[4]),
    ]
    for copy in moments_in:
        copy.start()
    rank = dirs.shape[3]
    depth = basis.shape[0]
    owned = update.shape[1] // 8
    stores = []
    basis_load.wait()
    for group, (start, rows) in enumerate(EXPAND_ROWS):
        loads[group].wait()
        kept = min(rows, owned - start)

        def tile(index, carry):
            lanes = pl.ds(pl.multiple_of(index * 256, 256), 256)
            total = lax.dot_general(
                dirs[:, :, pl.ds(start, rows), :].reshape(8 * rows, rank), basis[lanes, :],
                (((1,), (1,)), ((), ())), preferred_element_type=F32,
            )
            for half in range(2):
                for yl in range(2):
                    for x in range(4):
                        at = (yl * 4 + x) * rows
                        update[index * 2 + half, pl.ds(start * 8 + x * 2 + yl, kept, stride=8), :] = total[
                            at : at + kept, half * 128 : (half + 1) * 128
                        ]
            return carry

        lax.fori_loop(0, depth // 256, tile, 0)
        for column in range(depth // 128):
            place = pl.ds(start * 8, kept * 8)
            store = pltpu.make_async_copy(
                update.at[column, place], update_out.at[place, pl.ds(column * 128, 128)], store_sem.at[group, column]
            )
            store.start()
            stores.append(store)
        if group == 0:
            for copy_in, copy_out in zip(moments_in, moments_out):
                copy_in.wait()
                copy_out.start()
    for store in stores + moments_out:
        store.wait()


def expand(dirs, projector, first, second, owned):
    depth, rank = projector.shape[1:]
    in_hbm = pl.BlockSpec(memory_space=pl.ANY)
    moment = jax.ShapeDtypeStruct(first.shape, F32)
    return pl.pallas_call(
        expand_kernel,
        out_shape=(jax.ShapeDtypeStruct((owned * 8, depth), F32), moment, moment),
        in_specs=[in_hbm] * 4,
        out_specs=(in_hbm,) * 3,
        scratch_shapes=[
            pltpu.VMEM(dirs.shape, BF16),
            pltpu.VMEM((depth, rank), BF16),
            pltpu.VMEM((depth // 128, owned * 8, 128), F32),
            pltpu.VMEM(first.shape, F32),
            pltpu.VMEM(first.shape, F32),
            pltpu.SemaphoreType.DMA((len(EXPAND_ROWS),)),
            pltpu.SemaphoreType.DMA((len(EXPAND_ROWS), depth // 128)),
            pltpu.SemaphoreType.DMA((5,)),
        ],
        compiler_params=pltpu.CompilerParams(vmem_limit_bytes=60 << 20),
        name="expand",
    )(dirs, projector, first, second)


def local(activations, out_grads, projector, first_moment, second_moment):
    owned, rank = first_moment.shape[1:]
    flat = (owned * (rank // 128), 128)
    dirs, first, second = exchange(
        activations, jnp.swapaxes(out_grads, 1, 2), projector, first_moment.reshape(flat), second_moment.reshape(flat),
        owned,
    )
    update, first, second = expand(dirs, projector, first, second, owned)
    update = update.reshape(owned, 8, -1).transpose(1, 0, 2)[None]
    return update, first.reshape(first_moment.shape), second.reshape(second_moment.shape)


def solution(mesh):
    in_specs = (
        P(None, "dp", "fsdp"),
        P(None, "dp", "fsdp"),
        P(None, "fsdp", None),
        P(None, ("fsdp", "dp"), None),
        P(None, ("fsdp", "dp"), None),
    )
    out_specs = (
        P(None, None, "dp", "fsdp"),
        P(None, ("fsdp", "dp"), None),
        P(None, ("fsdp", "dp"), None),
    )
    return jax.shard_map(local, mesh=mesh, in_specs=in_specs, out_specs=out_specs, check_vma=False)
```

```python
import functools

import jax
import jax.numpy as jnp
from jax import lax
from jax.experimental import pallas as pl
from jax.experimental.pallas import tpu as pltpu
from jax.sharding import PartitionSpec as P

MESH = pl.DeviceIdType.MESH
F32, BF16 = jnp.float32, jnp.bfloat16

beta_first = 0.9
beta_second = 0.999
adam_count = 100.0
epsilon = 1e-08

CHUNKS = 8
RS_X_FIRST = (True, False, True, False, True, False, True, False)
AG_X_FIRST = (True, False, True, False, True, False, True, False)
DIR_X_FIRST = (True, False, True, False, True, False, True, False)
ORDER = (
    2, 3, 7, 0, 3, 6, 2, 1, 2, 3, 0, 7, 6, 3, 2, 1, 6, 0, 7, 5,
    2, 3, 6, 7, 4, 0, 2, 5, 3, 1, 7, 6, 4, 1, 2, 5, 7, 0, 3, 4,
    6, 1, 7, 5, 4, 2, 0, 6, 1, 7, 3, 2, 4, 5, 6, 3, 0, 7, 4, 1,
    2, 5, 6, 4, 3, 0, 1, 6, 7, 5, 0, 4, 1, 5, 4, 0, 1, 5, 4, 5,
)


def adam_direction(grad_low, first, second):
    first_next = beta_first * first + (1.0 - beta_first) * grad_low
    second_next = beta_second * second + (1.0 - beta_second) * grad_low * grad_low
    bias_first = 1.0 - beta_first**adam_count
    bias_second = 1.0 - beta_second**adam_count
    direction = first_next / bias_first / (jnp.sqrt(second_next / bias_second) + epsilon)
    return (first_next, second_next, direction.astype(BF16))


def wide(ref, *index):
    return ref[index].astype(F32)


def exchange_kernel(
    act_hbm, grads_hbm, basis_hbm, first_hbm, second_hbm,
    dirs_hbm, first_out, second_out,
    act, basis, grads_t, first, second, product,
    part, rs_a, rs_s, rs_b, projected,
    terms, core_in, z_out, z_in, y_out, y_in, dirs,
    load_sem, store_sem, send_sem, recv_sem,
):
    dp, fs = lax.axis_index("dp"), lax.axis_index("fsdp")
    yh, z, core = dp // 8, (dp // 2) % 4, dp % 2
    x, yl = fs // 2, fs % 2
    chunk = basis.shape[1] // CHUNKS
    row_tiles = basis.shape[1] // 128
    owned = first.shape[0] // row_tiles
    padded = dirs.shape[3]
    tokens = part.shape[3]
    features = act.shape[0]

    to_x = [None] + [(x + d) % 4 for d in (1, 2, 3)]
    to_z = [None] + [(z + d) % 4 for d in (1, 2, 3)]
    x_peers = [None] + [(dp, to_x[d] * 2 + yl) for d in (1, 2, 3)]
    z_peers = [None] + [(yh * 8 + to_z[d] * 2 + core, fs) for d in (1, 2, 3)]
    y_near = (dp, x * 2 + 1 - yl)
    y_far = ((1 - yh) * 8 + z * 2 + core, fs)
    sibling = (yh * 8 + z * 2 + 1 - core, fs)

    half = features // 2
    pair = 2 * chunk
    act_loads = [
        pltpu.make_async_copy(act_hbm.at[0, pl.ds(i * half, half)], act.at[pl.ds(i * half, half)], load_sem.at[i])
        for i in range(2)
    ]
    basis_loads = [
        pltpu.make_async_copy(
            basis_hbm.at[0, :, pl.ds(i * pair, pair)], basis.at[:, pl.ds(i * pair, pair)], load_sem.at[2 + i]
        )
        for i in range(CHUNKS // 2)
    ]
    grads_load = pltpu.make_async_copy(grads_hbm.at[0], grads_t, load_sem.at[2 + CHUNKS // 2])
    moment_loads = [
        pltpu.make_async_copy(first_hbm, first, load_sem.at[3 + CHUNKS // 2]),
        pltpu.make_async_copy(second_hbm, second, load_sem.at[4 + CHUNKS // 2]),
    ]
    pairs = list(dict.fromkeys(c // 2 for c in ORDER))
    basis_loads[pairs[0]].start()
    for load in act_loads + [basis_loads[i] for i in pairs[1:]] + [grads_load] + moment_loads:
        load.start()

    barrier = pltpu.get_barrier_semaphore()
    peers = x_peers[1:] + z_peers[1:] + [y_near, y_far, sibling]
    for peer in peers:
        pl.semaphore_signal(barrier, inc=1, device_id=peer, device_id_type=MESH)

    sent = [[] for _ in range(CHUNKS)]

    def remote(source, target, c, slot, peer):
        return pltpu.make_async_remote_copy(
            src_ref=source, dst_ref=target, send_sem=send_sem.at[c, slot], recv_sem=recv_sem.at[c, slot],
            device_id=peer, device_id_type=MESH,
        )

    def send(source, target, c, slot, peer):
        copy = remote(source, target, c, slot, peer)
        copy.start()
        sent[c].append(copy)

    def arrived(target, c, slot, peer):
        remote(target, target, c, slot, peer).wait_recv()


    def project(c):
        basis_loads[c // 2].wait()
        for index in range(2):
            if "act" not in waited:
                act_loads[index].wait()
            value = jnp.dot(
                act[index * half : (index + 1) * half, :], basis[:, c * chunk : (c + 2) * chunk],
                preferred_element_type=F32,
            ).astype(BF16)
            for which in range(2):
                part[c + which, index] = value[:, which * chunk : (which + 1) * chunk].reshape(4, tokens, chunk)
        waited.add("act")

    def reduce_first(c):
        if RS_X_FIRST[c]:
            for d in (2, 1, 3):
                send(part.at[c, :, to_x[d]], rs_a.at[c, pl.ds((d - 1) * 2, 2)], c, d - 1, x_peers[d])
        else:
            send(part.at[c, 1 - yl], rs_a.at[c, pl.ds(0, 4)], c, 3, y_near)

    def reduce_second(c):
        if RS_X_FIRST[c]:
            for d in (1, 3, 2):
                arrived(rs_a.at[c, pl.ds((d - 1) * 2, 2)], c, d - 1, x_peers[d])
            other = 1 - yl

            total = wide(part, c, other, x)
            for d in range(3):
                total += wide(rs_a, c, 2 * d + other)
            rs_s[c, 0] = total.astype(BF16)
            send(rs_s.at[c, 0], rs_b.at[c, 0], c, 3, y_near)
        else:
            arrived(rs_a.at[c, pl.ds(0, 4)], c, 3, y_near)
            for d in (2, 1, 3):
                to = to_x[d]
                rs_s[c, d - 1] = (wide(part, c, yl, to) + wide(rs_a, c, to)).astype(BF16)
                send(rs_s.at[c, d - 1], rs_b.at[c, d - 1], c, d - 1, x_peers[d])

    def reduce_last(c):
        if RS_X_FIRST[c]:
            arrived(rs_b.at[c, 0], c, 3, y_near)
            total = wide(part, c, yl, x) + wide(rs_b, c, 0)
            for d in range(3):
                total += wide(rs_a, c, 2 * d + yl)
        else:
            for d in (1, 3, 2):
                arrived(rs_b.at[c, d - 1], c, d - 1, x_peers[d])
            total = wide(part, c, yl, x) + wide(rs_a, c, x)
            for d in range(3):
                total += wide(rs_b, c, d)
        projected[c, yl, x] = total.astype(BF16)

    def gather_first(buffer, target, c, slot, x_first):
        mine, there = buffer.at[c, yl, x], target.at[yl, x]
        send(mine, there if x_first else mine, c, slot + 3, y_near)
        for d in (2, 1, 3):
            send(mine, mine if x_first else there, c, slot + d - 1, x_peers[d])

    def gather_second(buffer, target, c, slot, x_first):
        if x_first:
            for d in (1, 3, 2):
                block = (yl, to_x[4 - d])
                arrived(buffer.at[(c,) + block], c, slot + d - 1, x_peers[d])
                send(buffer.at[(c,) + block], target.at[block], c, slot + 3 + d, y_near)
        else:
            block = (1 - yl, x)
            arrived(buffer.at[(c,) + block], c, slot + 3, y_near)
            for d in (2, 1, 3):
                send(buffer.at[(c,) + block], target.at[block], c, slot + 3 + d, x_peers[d])

    def gather_last(target, c, slot, x_first):
        if x_first:
            arrived(target.at[1 - yl, x], c, slot + 3, y_near)
            for d in (1, 3, 2):
                arrived(target.at[1 - yl, to_x[4 - d]], c, slot + 3 + d, y_near)
        else:
            for d in (1, 3, 2):
                arrived(target.at[yl, to_x[4 - d]], c, slot + d - 1, x_peers[d])
            for d in (1, 3, 2):
                arrived(target.at[1 - yl, to_x[4 - d]], c, slot + 3 + d, x_peers[d])

    def gradient(first_c):
        rows_all = grads_t.shape[0]
        tile = rows_all // 4

        def one(index, carry):
            rows = pl.ds(pl.multiple_of(index * tile, tile), tile)
            right = jnp.concatenate([projected[first_c + k].reshape(features, chunk) for k in range(2)], axis=1)
            product[rows, :] = jnp.dot(grads_t[rows, :], right, preferred_element_type=F32)
            return carry

        lax.fori_loop(0, 4, one, 0)

        def two(pair, carry):
            for which in range(2):
                shift = which * owned % 8
                start = pl.multiple_of(pair * (2 * owned) + which * owned - shift, 8)
                value = product[pl.ds(start, padded + 8), :]
                value = value[shift : shift + padded].astype(BF16)
                for k in range(2):
                    terms[first_c + k, which, pair // 4, pair % 4] = value[:, k * chunk : (k + 1) * chunk]
            return carry

        lax.fori_loop(0, 8, two, 0)
        for c in (first_c, first_c + 1):
            send(terms.at[c, 1 - core], core_in.at[c], c, 11, sibling)

    def core_sum(c):
        arrived(core_in.at[c], c, 11, sibling)
        for h, slot in ((1 - yh, 11), (yh, 14)):
            for d in (2, 1, 3):
                to = to_z[d]
                z_out[c, d - 1, h] = (wide(terms, c, core, h, to) + wide(core_in, c, h, to)).astype(BF16)
                send(z_out.at[c, d - 1, h], z_in.at[c, d - 1, h], c, slot + d, z_peers[d])

    def z_arrived(c, h, slot):
        for d in (1, 3, 2):
            arrived(z_in.at[c, d - 1, h], c, slot + d, z_peers[d])

    def z_sum(c, h):
        total = wide(terms, c, core, h, z) + wide(core_in, c, h, z)
        for d in range(3):
            total += wide(z_in, c, d, h)
        return total

    def z_stage(c):
        z_arrived(c, 1 - yh, 11)
        y_out[c] = z_sum(c, 1 - yh).astype(BF16)
        send(y_out.at[c], y_in.at[c], c, 18, y_far)

    def adam(c):
        if "moments" not in waited:
            for load in moment_loads:
                load.wait()
            waited.add("moments")
        z_arrived(c, yh, 14)
        arrived(y_in.at[c], c, 18, y_far)

        low = (z_sum(c, yh) + wide(y_in, c))[:owned]
        for part_of in range(chunk // 128):
            lanes = slice(part_of * 128, (part_of + 1) * 128)
            here = pl.ds(c * (chunk // 128) + part_of, owned, stride=row_tiles)
            first_next, second_next, direction = adam_direction(low[:, lanes], first[here, :], second[here, :])
            first[here, :] = first_next
            second[here, :] = second_next
            dirs[c, yl, x, :owned, lanes] = direction

    def dirs_out(c):
        return dirs_hbm.at[:, :, :, pl.ds(c * chunk, chunk)]

    def out_copies(c):
        if DIR_X_FIRST[c]:
            return pltpu.make_async_copy(dirs.at[c, yl], dirs_out(c).at[yl], store_sem.at[c, 0])
        return pltpu.make_async_copy(dirs.at[c, :, x], dirs_out(c).at[:, x], store_sem.at[c, 0])

    barrier_done, projected_pairs, waited, gathered = [], set(), set(), set()

    def stage(s, c):
        if s == 0:
            if c // 2 not in projected_pairs:
                project(c // 2 * 2)
                projected_pairs.add(c // 2)
            if not barrier_done:
                pl.semaphore_wait(barrier, len(peers))
                barrier_done.append(True)
            reduce_first(c)
        elif s == 1:
            reduce_second(c)
        elif s == 2:
            reduce_last(c)
            gather_first(projected, projected.at[c], c, 4, AG_X_FIRST[c])
        elif s == 3:
            gather_second(projected, projected.at[c], c, 4, AG_X_FIRST[c])
        elif s == 4:
            gather_last(projected.at[c], c, 4, AG_X_FIRST[c])
            if "grads" not in waited:
                grads_load.wait()
                waited.add("grads")
            if c ^ 1 in gathered:
                gradient(c // 2 * 2)
            gathered.add(c)
        elif s == 5:
            done = sent[c][:-1]
            core_sum(c)
            for copy in done:
                copy.wait_send()
            del sent[c][: len(done)]
        elif s == 6:
            z_stage(c)
        elif s == 7:
            adam(c)
            gather_first(dirs, dirs_out(c), c, 19, DIR_X_FIRST[c])
        elif s == 8:
            done = sent[c][:8]
            gather_second(dirs, dirs_out(c), c, 19, DIR_X_FIRST[c])
            out_copies(c).start()
            for copy in done:
                copy.wait_send()
            del sent[c][: len(done)]
        else:
            gather_last(dirs_out(c), c, 19, DIR_X_FIRST[c])

    order, turns = [], [0] * CHUNKS
    for c in ORDER:
        order.append((None, c, turns[c]))
        turns[c] += 1
    moments = [
        pltpu.make_async_copy(first, first_out, store_sem.at[CHUNKS, 0]),
        pltpu.make_async_copy(second, second_out, store_sem.at[CHUNKS + 1, 0]),
    ]
    last_adam = [c for _, c, s in order if s == 7][-1]
    for _, c, s in order:
        stage(s, c)
        if s == 7 and c == last_adam:
            for copy in moments:
                copy.start()
    for c in range(CHUNKS):
        for copy in sent[c]:
            copy.wait_send()
    for c in range(CHUNKS):
        out_copies(c).wait()
    for copy in moments:
        copy.wait()


def exchange(activations, grads_t, projector, first, second, owned):
    features = activations.shape[1]
    width = grads_t.shape[1]
    depth, rank = projector.shape[1:]
    padded = -(-owned // 16) * 16
    chunk = rank // CHUNKS
    tokens = features // 8
    in_hbm = pl.BlockSpec(memory_space=pl.ANY)
    C = CHUNKS
    scratch = [
        pltpu.VMEM((features, depth), BF16),
        pltpu.VMEM((depth, rank), BF16),
        pltpu.VMEM((width, features), BF16),
        pltpu.VMEM(first.shape, F32),
        pltpu.VMEM(first.shape, F32),
        pltpu.VMEM((width + 16, 2 * chunk), F32),
        pltpu.VMEM((C, 2, 4, tokens, chunk), BF16),
        pltpu.VMEM((C, 6, tokens, chunk), BF16),
        pltpu.VMEM((C, 3, tokens, chunk), BF16),
        pltpu.VMEM((C, 3, tokens, chunk), BF16),
        pltpu.VMEM((C, 2, 4, tokens, chunk), BF16),
        pltpu.VMEM((C, 2, 2, 4, padded, chunk), BF16),
        pltpu.VMEM((C, 2, 4, padded, chunk), BF16),
        pltpu.VMEM((C, 3, 2, padded, chunk), BF16),
        pltpu.VMEM((C, 3, 2, padded, chunk), BF16),
        pltpu.VMEM((C, padded, chunk), BF16),
        pltpu.VMEM((C, padded, chunk), BF16),
        pltpu.VMEM((C, 2, 4, padded, chunk), BF16),
        pltpu.SemaphoreType.DMA((5 + C // 2,)),
        pltpu.SemaphoreType.DMA((C + 2, 2)),
        pltpu.SemaphoreType.DMA((C, 26)),
        pltpu.SemaphoreType.DMA((C, 26)),
    ]
    return pl.pallas_call(
        exchange_kernel,
        out_shape=(
            jax.ShapeDtypeStruct((2, 4, padded, rank), BF16),
            jax.ShapeDtypeStruct(first.shape, F32),
            jax.ShapeDtypeStruct(first.shape, F32),
        ),
        in_specs=[in_hbm] * 5,
        out_specs=(in_hbm,) * 3,
        scratch_shapes=scratch,
        compiler_params=pltpu.CompilerParams(
            collective_id=0, has_side_effects=True, vmem_limit_bytes=60 << 20
        ),
        name="exchange",
    )(activations, grads_t, projector, first, second)


EXPAND_ROWS = ((0, 48), (48, 80), (128, 48))
EXPAND_LANES = 512


def expand_kernel(
    dirs_hbm, basis_hbm, first_in, second_in, update_out, first_out, second_out,
    dirs, basis, update, first, second, load_sem, basis_sem, store_sem, sem,
):
    rank = dirs.shape[3]
    depth = basis.shape[0]
    owned = update.shape[1] // 8
    tiles = [pl.ds(lane, EXPAND_LANES) for lane in range(0, depth, EXPAND_LANES)]
    basis_loads = [
        pltpu.make_async_copy(basis_hbm.at[0, lanes], basis.at[lanes], basis_sem.at[index])
        for index, lanes in enumerate(tiles)
    ]
    loads = [
        pltpu.make_async_copy(dirs_hbm.at[:, :, pl.ds(*rows)], dirs.at[:, :, pl.ds(*rows)], load_sem.at[group])
        for group, rows in enumerate(EXPAND_ROWS)
    ]
    basis_loads[0].start()
    for load in loads[:1] + basis_loads[1:] + loads[1:]:
        load.start()
    moments_in = [
        pltpu.make_async_copy(first_in, first, sem.at[0]),
        pltpu.make_async_copy(second_in, second, sem.at[1]),
    ]
    moments_out = [
        pltpu.make_async_copy(first, first_out, sem.at[2]),
        pltpu.make_async_copy(second, second_out, sem.at[3]),
    ]
    for copy in moments_in:
        copy.start()
    stores = []
    for group, (start, rows) in enumerate(EXPAND_ROWS):
        loads[group].wait()
        kept = min(rows, owned - start)

        for index, lanes in enumerate(tiles):
            if group == 0:
                basis_loads[index].wait()
            total = lax.dot_general(
                dirs[:, :, pl.ds(start, rows), :].reshape(8 * rows, rank), basis[lanes, :],
                (((1,), (1,)), ((), ())), preferred_element_type=F32,
            )
            for part_of in range(EXPAND_LANES // 128):
                column = index * (EXPAND_LANES // 128) + part_of
                for yl in range(2):
                    for x in range(4):
                        at = (yl * 4 + x) * rows
                        update[column, pl.ds(start * 8 + x * 2 + yl, kept, stride=8), :] = total[
                            at : at + kept, part_of * 128 : (part_of + 1) * 128
                        ]
        for column in range(depth // 128):
            place = pl.ds(start * 8, kept * 8)
            store = pltpu.make_async_copy(
                update.at[column, place], update_out.at[place, pl.ds(column * 128, 128)], store_sem.at[group, column]
            )
            store.start()
            stores.append(store)
        if group == 0:
            for copy_in, copy_out in zip(moments_in, moments_out):
                copy_in.wait()
                copy_out.start()
    for store in stores + moments_out:
        store.wait()


def expand(dirs, projector, first, second, owned):
    depth, rank = projector.shape[1:]
    in_hbm = pl.BlockSpec(memory_space=pl.ANY)
    moment = jax.ShapeDtypeStruct(first.shape, F32)
    return pl.pallas_call(
        expand_kernel,
        out_shape=(jax.ShapeDtypeStruct((owned * 8, depth), F32), moment, moment),
        in_specs=[in_hbm] * 4,
        out_specs=(in_hbm,) * 3,
        scratch_shapes=[
            pltpu.VMEM(dirs.shape, BF16),
            pltpu.VMEM((depth, rank), BF16),
            pltpu.VMEM((depth // 128, owned * 8, 128), F32),
            pltpu.VMEM(first.shape, F32),
            pltpu.VMEM(first.shape, F32),
            pltpu.SemaphoreType.DMA((len(EXPAND_ROWS),)),
            pltpu.SemaphoreType.DMA((depth // EXPAND_LANES,)),
            pltpu.SemaphoreType.DMA((len(EXPAND_ROWS), depth // 128)),
            pltpu.SemaphoreType.DMA((4,)),
        ],
        compiler_params=pltpu.CompilerParams(vmem_limit_bytes=60 << 20),
        name="expand",
    )(dirs, projector, first, second)


def local(activations, out_grads, projector, first_moment, second_moment):
    owned, rank = first_moment.shape[1:]
    flat = (owned * (rank // 128), 128)
    dirs, first, second = exchange(
        activations, jnp.swapaxes(out_grads, 1, 2), projector, first_moment.reshape(flat), second_moment.reshape(flat),
        owned,
    )
    update, first, second = expand(dirs, projector, first, second, owned)
    update = update.reshape(owned, 8, -1).transpose(1, 0, 2)[None]
    return update, first.reshape(first_moment.shape), second.reshape(second_moment.shape)


def solution(mesh):
    in_specs = (
        P(None, "dp", "fsdp"),
        P(None, "dp", "fsdp"),
        P(None, "fsdp", None),
        P(None, ("fsdp", "dp"), None),
        P(None, ("fsdp", "dp"), None),
    )
    out_specs = (
        P(None, None, "dp", "fsdp"),
        P(None, ("fsdp", "dp"), None),
        P(None, ("fsdp", "dp"), None),
    )
    return jax.shard_map(local, mesh=mesh, in_specs=in_specs, out_specs=out_specs, check_vma=False)
```

```python
import functools

import jax
import jax.numpy as jnp
from jax import lax
from jax.experimental import pallas as pl
from jax.experimental.pallas import tpu as pltpu
from jax.sharding import PartitionSpec as P

MESH = pl.DeviceIdType.MESH
F32, BF16 = jnp.float32, jnp.bfloat16

beta_first = 0.9
beta_second = 0.999
adam_count = 100.0
epsilon = 1e-08

CHUNKS = 8
RS_X_FIRST = (True, False, True, False, True, False, True, False)
AG_X_FIRST = (True, False, True, False, True, False, True, False)
DIR_X_FIRST = (True, False, True, False, True, False, True, False)
ORDER = (
    2, 3, 7, 0, 3, 6, 2, 1, 2, 3, 0, 7, 6, 3, 2, 1, 6, 0, 7, 5,
    2, 3, 6, 7, 4, 0, 2, 5, 3, 1, 7, 6, 4, 1, 2, 5, 7, 0, 3, 4,
    6, 1, 7, 5, 4, 2, 0, 6, 1, 7, 3, 2, 4, 5, 6, 3, 0, 7, 4, 1,
    2, 5, 6, 4, 3, 0, 1, 6, 7, 5, 0, 4, 1, 5, 4, 0, 1, 5, 4, 5,
)


def adam_direction(grad_low, first, second):
    first_next = beta_first * first + (1.0 - beta_first) * grad_low
    second_next = beta_second * second + (1.0 - beta_second) * grad_low * grad_low
    bias_first = 1.0 - beta_first**adam_count
    bias_second = 1.0 - beta_second**adam_count
    direction = first_next / bias_first / (jnp.sqrt(second_next / bias_second) + epsilon)
    return (first_next, second_next, direction.astype(BF16))


def wide(ref, *index):
    return ref[index].astype(F32)


def exchange_kernel(
    act_hbm, grads_hbm, basis_hbm, first_hbm, second_hbm,
    dirs_hbm, first_out, second_out,
    act, basis, grads_t, first, second, product,
    part, rs_a, rs_s, rs_b, projected,
    terms, core_in, z_out, z_in, y_out, y_in, dirs,
    load_sem, store_sem, send_sem, recv_sem,
):
    dp, fs = lax.axis_index("dp"), lax.axis_index("fsdp")
    yh, z, core = dp // 8, (dp // 2) % 4, dp % 2
    x, yl = fs // 2, fs % 2
    chunk = basis.shape[1] // CHUNKS
    row_tiles = basis.shape[1] // 128
    owned = first.shape[0] // row_tiles
    padded = dirs.shape[3]
    tokens = part.shape[3]
    features = act.shape[0]

    to_x = [None] + [(x + d) % 4 for d in (1, 2, 3)]
    to_z = [None] + [(z + d) % 4 for d in (1, 2, 3)]
    x_peers = [None] + [(dp, to_x[d] * 2 + yl) for d in (1, 2, 3)]
    z_peers = [None] + [(yh * 8 + to_z[d] * 2 + core, fs) for d in (1, 2, 3)]
    y_near = (dp, x * 2 + 1 - yl)
    y_far = ((1 - yh) * 8 + z * 2 + core, fs)
    sibling = (yh * 8 + z * 2 + 1 - core, fs)

    half = features // 2
    pair = 2 * chunk
    act_loads = [
        pltpu.make_async_copy(act_hbm.at[0, pl.ds(i * half, half)], act.at[pl.ds(i * half, half)], load_sem.at[i])
        for i in range(2)
    ]
    basis_loads = [
        pltpu.make_async_copy(
            basis_hbm.at[0, :, pl.ds(i * pair, pair)], basis.at[:, pl.ds(i * pair, pair)], load_sem.at[2 + i]
        )
        for i in range(CHUNKS // 2)
    ]
    grads_load = pltpu.make_async_copy(grads_hbm.at[0], grads_t, load_sem.at[2 + CHUNKS // 2])
    moment_loads = [
        pltpu.make_async_copy(first_hbm, first, load_sem.at[3 + CHUNKS // 2]),
        pltpu.make_async_copy(second_hbm, second, load_sem.at[4 + CHUNKS // 2]),
    ]
    pairs = list(dict.fromkeys(c // 2 for c in ORDER))
    basis_loads[pairs[0]].start()
    for load in act_loads + [basis_loads[i] for i in pairs[1:]] + [grads_load] + moment_loads:
        load.start()

    barrier = pltpu.get_barrier_semaphore()
    peers = x_peers[1:] + z_peers[1:] + [y_near, y_far, sibling]
    for peer in peers:
        pl.semaphore_signal(barrier, inc=1, device_id=peer, device_id_type=MESH)

    sent = [[] for _ in range(CHUNKS)]

    def remote(source, target, c, slot, peer):
        return pltpu.make_async_remote_copy(
            src_ref=source, dst_ref=target, send_sem=send_sem.at[c, slot], recv_sem=recv_sem.at[c, slot],
            device_id=peer, device_id_type=MESH,
        )

    def send(source, target, c, slot, peer):
        copy = remote(source, target, c, slot, peer)
        copy.start()
        sent[c].append(copy)

    def arrived(target, c, slot, peer):
        remote(target, target, c, slot, peer).wait_recv()


    def project(c):
        basis_loads[c // 2].wait()
        for index in range(2):
            if "act" not in waited:
                act_loads[index].wait()
            value = jnp.dot(
                act[index * half : (index + 1) * half, :], basis[:, c * chunk : (c + 2) * chunk],
                preferred_element_type=F32,
            ).astype(BF16)
            for which in range(2):
                part[c + which, index] = value[:, which * chunk : (which + 1) * chunk].reshape(4, tokens, chunk)
        waited.add("act")

    def reduce_first(c):
        if RS_X_FIRST[c]:
            for d in (2, 1, 3):
                send(part.at[c, :, to_x[d]], rs_a.at[c, pl.ds((d - 1) * 2, 2)], c, d - 1, x_peers[d])
        else:
            send(part.at[c, 1 - yl], rs_a.at[c, pl.ds(0, 4)], c, 3, y_near)

    def reduce_second(c):
        if RS_X_FIRST[c]:
            for d in (1, 3, 2):
                arrived(rs_a.at[c, pl.ds((d - 1) * 2, 2)], c, d - 1, x_peers[d])
            other = 1 - yl

            total = wide(part, c, other, x)
            for d in range(3):
                total += wide(rs_a, c, 2 * d + other)
            rs_s[c, 0] = total.astype(BF16)
            send(rs_s.at[c, 0], rs_b.at[c, 0], c, 3, y_near)
        else:
            arrived(rs_a.at[c, pl.ds(0, 4)], c, 3, y_near)
            for d in (2, 1, 3):
                to = to_x[d]
                rs_s[c, d - 1] = (wide(part, c, yl, to) + wide(rs_a, c, to)).astype(BF16)
                send(rs_s.at[c, d - 1], rs_b.at[c, d - 1], c, d - 1, x_peers[d])

    def reduce_last(c):
        if RS_X_FIRST[c]:
            arrived(rs_b.at[c, 0], c, 3, y_near)
            total = wide(part, c, yl, x) + wide(rs_b, c, 0)
            for d in range(3):
                total += wide(rs_a, c, 2 * d + yl)
        else:
            for d in (1, 3, 2):
                arrived(rs_b.at[c, d - 1], c, d - 1, x_peers[d])
            total = wide(part, c, yl, x) + wide(rs_a, c, x)
            for d in range(3):
                total += wide(rs_b, c, d)
        projected[c, yl, x] = total.astype(BF16)

    def gather_first(buffer, target, c, slot, x_first):
        mine, there = buffer.at[c, yl, x], target.at[yl, x]
        send(mine, there if x_first else mine, c, slot + 3, y_near)
        for d in (2, 1, 3):
            send(mine, mine if x_first else there, c, slot + d - 1, x_peers[d])

    def gather_second(buffer, target, c, slot, x_first):
        if x_first:
            for d in (1, 3, 2):
                block = (yl, to_x[4 - d])
                arrived(buffer.at[(c,) + block], c, slot + d - 1, x_peers[d])
                send(buffer.at[(c,) + block], target.at[block], c, slot + 3 + d, y_near)
        else:
            block = (1 - yl, x)
            arrived(buffer.at[(c,) + block], c, slot + 3, y_near)
            for d in (2, 1, 3):
                send(buffer.at[(c,) + block], target.at[block], c, slot + 3 + d, x_peers[d])

    def gather_last(target, c, slot, x_first):
        if x_first:
            arrived(target.at[1 - yl, x], c, slot + 3, y_near)
            for d in (1, 3, 2):
                arrived(target.at[1 - yl, to_x[4 - d]], c, slot + 3 + d, y_near)
        else:
            for d in (1, 3, 2):
                arrived(target.at[yl, to_x[4 - d]], c, slot + d - 1, x_peers[d])
            for d in (1, 3, 2):
                arrived(target.at[1 - yl, to_x[4 - d]], c, slot + 3 + d, x_peers[d])

    def gradient(first_c):
        rows_all = grads_t.shape[0]
        tile = rows_all // 4

        def one(index, carry):
            rows = pl.ds(pl.multiple_of(index * tile, tile), tile)
            right = jnp.concatenate([projected[first_c + k].reshape(features, chunk) for k in range(2)], axis=1)
            product[rows, :] = jnp.dot(grads_t[rows, :], right, preferred_element_type=F32)
            return carry

        lax.fori_loop(0, 4, one, 0)

        def blocks_of(which):
            shift = which * owned % 8

            def two(block, carry):
                start = pl.multiple_of(block * (2 * owned) + which * owned - shift, 8)
                value = product[pl.ds(start, padded + 8), :]
                value = value[shift : shift + padded].astype(BF16)
                for k in range(2):
                    terms[first_c + k, which, block // 4, block % 4] = value[:, k * chunk : (k + 1) * chunk]
                return carry

            lax.fori_loop(0, 8, two, 0)

        lax.cond(core == 0, lambda: blocks_of(1), lambda: blocks_of(0))
        for c in (first_c, first_c + 1):
            send(terms.at[c, 1 - core], core_in.at[c], c, 11, sibling)
        lax.cond(core == 0, lambda: blocks_of(0), lambda: blocks_of(1))

    def core_sum(c):
        arrived(core_in.at[c], c, 11, sibling)
        for h, slot in ((1 - yh, 11), (yh, 14)):
            for d in (2, 1, 3):
                to = to_z[d]
                z_out[c, d - 1, h] = (wide(terms, c, core, h, to) + wide(core_in, c, h, to)).astype(BF16)
                send(z_out.at[c, d - 1, h], z_in.at[c, d - 1, h], c, slot + d, z_peers[d])

    def z_arrived(c, h, slot):
        for d in (1, 3, 2):
            arrived(z_in.at[c, d - 1, h], c, slot + d, z_peers[d])

    def z_sum(c, h):
        total = wide(terms, c, core, h, z) + wide(core_in, c, h, z)
        for d in range(3):
            total += wide(z_in, c, d, h)
        return total

    def z_stage(c):
        z_arrived(c, 1 - yh, 11)
        y_out[c] = z_sum(c, 1 - yh).astype(BF16)
        send(y_out.at[c], y_in.at[c], c, 18, y_far)

    def adam(c):
        if "moments" not in waited:
            for load in moment_loads:
                load.wait()
            waited.add("moments")
        z_arrived(c, yh, 14)
        arrived(y_in.at[c], c, 18, y_far)

        low = (z_sum(c, yh) + wide(y_in, c))[:owned]
        for part_of in range(chunk // 128):
            lanes = slice(part_of * 128, (part_of + 1) * 128)
            here = pl.ds(c * (chunk // 128) + part_of, owned, stride=row_tiles)
            first_next, second_next, direction = adam_direction(low[:, lanes], first[here, :], second[here, :])
            first[here, :] = first_next
            second[here, :] = second_next
            dirs[c, yl, x, :owned, lanes] = direction

    def dirs_out(c):
        return dirs_hbm.at[:, :, :, pl.ds(c * chunk, chunk)]

    def out_copies(c):
        if DIR_X_FIRST[c]:
            return pltpu.make_async_copy(dirs.at[c, yl], dirs_out(c).at[yl], store_sem.at[c, 0])
        return pltpu.make_async_copy(dirs.at[c, :, x], dirs_out(c).at[:, x], store_sem.at[c, 0])

    barrier_done, projected_pairs, waited, gathered = [], set(), set(), set()

    def stage(s, c):
        if s == 0:
            if c // 2 not in projected_pairs:
                project(c // 2 * 2)
                projected_pairs.add(c // 2)
            if not barrier_done:
                pl.semaphore_wait(barrier, len(peers))
                barrier_done.append(True)
            reduce_first(c)
        elif s == 1:
            reduce_second(c)
        elif s == 2:
            reduce_last(c)
            gather_first(projected, projected.at[c], c, 4, AG_X_FIRST[c])
        elif s == 3:
            gather_second(projected, projected.at[c], c, 4, AG_X_FIRST[c])
        elif s == 4:
            gather_last(projected.at[c], c, 4, AG_X_FIRST[c])
            if "grads" not in waited:
                grads_load.wait()
                waited.add("grads")
            if c ^ 1 in gathered:
                gradient(c // 2 * 2)
            gathered.add(c)
        elif s == 5:
            done = sent[c][:-1]
            core_sum(c)
            for copy in done:
                copy.wait_send()
            del sent[c][: len(done)]
        elif s == 6:
            z_stage(c)
        elif s == 7:
            adam(c)
            gather_first(dirs, dirs_out(c), c, 19, DIR_X_FIRST[c])
        elif s == 8:
            done = sent[c][:8]
            gather_second(dirs, dirs_out(c), c, 19, DIR_X_FIRST[c])
            out_copies(c).start()
            for copy in done:
                copy.wait_send()
            del sent[c][: len(done)]
        else:
            gather_last(dirs_out(c), c, 19, DIR_X_FIRST[c])
            for copy in sent[c]:
                copy.wait_send()
            out_copies(c).wait()

    order, turns = [], [0] * CHUNKS
    for c in ORDER:
        order.append((None, c, turns[c]))
        turns[c] += 1
    moments = [
        pltpu.make_async_copy(first, first_out, store_sem.at[CHUNKS, 0]),
        pltpu.make_async_copy(second, second_out, store_sem.at[CHUNKS + 1, 0]),
    ]
    last_adam = [c for _, c, s in order if s == 7][-1]
    for _, c, s in order:
        stage(s, c)
        if s == 7 and c == last_adam:
            for copy in moments:
                copy.start()
    for copy in moments:
        copy.wait()


def exchange(activations, grads_t, projector, first, second, owned):
    features = activations.shape[1]
    width = grads_t.shape[1]
    depth, rank = projector.shape[1:]
    padded = -(-owned // 16) * 16
    chunk = rank // CHUNKS
    tokens = features // 8
    in_hbm = pl.BlockSpec(memory_space=pl.ANY)
    C = CHUNKS
    scratch = [
        pltpu.VMEM((features, depth), BF16),
        pltpu.VMEM((depth, rank), BF16),
        pltpu.VMEM((width, features), BF16),
        pltpu.VMEM(first.shape, F32),
        pltpu.VMEM(first.shape, F32),
        pltpu.VMEM((width + 16, 2 * chunk), F32),
        pltpu.VMEM((C, 2, 4, tokens, chunk), BF16),
        pltpu.VMEM((C, 6, tokens, chunk), BF16),
        pltpu.VMEM((C, 3, tokens, chunk), BF16),
        pltpu.VMEM((C, 3, tokens, chunk), BF16),
        pltpu.VMEM((C, 2, 4, tokens, chunk), BF16),
        pltpu.VMEM((C, 2, 2, 4, padded, chunk), BF16),
        pltpu.VMEM((C, 2, 4, padded, chunk), BF16),
        pltpu.VMEM((C, 3, 2, padded, chunk), BF16),
        pltpu.VMEM((C, 3, 2, padded, chunk), BF16),
        pltpu.VMEM((C, padded, chunk), BF16),
        pltpu.VMEM((C, padded, chunk), BF16),
        pltpu.VMEM((C, 2, 4, padded, chunk), BF16),
        pltpu.SemaphoreType.DMA((5 + C // 2,)),
        pltpu.SemaphoreType.DMA((C + 2, 2)),
        pltpu.SemaphoreType.DMA((C, 26)),
        pltpu.SemaphoreType.DMA((C, 26)),
    ]
    return pl.pallas_call(
        exchange_kernel,
        out_shape=(
            jax.ShapeDtypeStruct((2, 4, padded, rank), BF16),
            jax.ShapeDtypeStruct(first.shape, F32),
            jax.ShapeDtypeStruct(first.shape, F32),
        ),
        in_specs=[in_hbm] * 5,
        out_specs=(in_hbm,) * 3,
        scratch_shapes=scratch,
        compiler_params=pltpu.CompilerParams(
            collective_id=0, has_side_effects=True, vmem_limit_bytes=60 << 20
        ),
        name="exchange",
    )(activations, grads_t, projector, first, second)


EXPAND_ROWS = ((0, 64), (64, 80), (144, 32))
EXPAND_LANES = 512


def expand_kernel(
    dirs_hbm, basis_hbm, first_in, second_in, update_out, first_out, second_out,
    dirs, basis, update, first, second, load_sem, basis_sem, store_sem, sem,
):
    rank = dirs.shape[3]
    depth = basis.shape[0]
    owned = update.shape[1] // 8
    tiles = [pl.ds(lane, EXPAND_LANES) for lane in range(0, depth, EXPAND_LANES)]
    basis_loads = [
        pltpu.make_async_copy(basis_hbm.at[0, lanes], basis.at[lanes], basis_sem.at[index])
        for index, lanes in enumerate(tiles)
    ]
    loads = [
        pltpu.make_async_copy(dirs_hbm.at[:, :, pl.ds(*rows)], dirs.at[:, :, pl.ds(*rows)], load_sem.at[group])
        for group, rows in enumerate(EXPAND_ROWS)
    ]
    basis_loads[0].start()
    for load in loads[:1] + basis_loads[1:] + loads[1:]:
        load.start()
    moments_in = [
        pltpu.make_async_copy(first_in, first, sem.at[0]),
        pltpu.make_async_copy(second_in, second, sem.at[1]),
    ]
    moments_out = [
        pltpu.make_async_copy(first, first_out, sem.at[2]),
        pltpu.make_async_copy(second, second_out, sem.at[3]),
    ]
    for copy in moments_in:
        copy.start()
    stores = []
    for group, (start, rows) in enumerate(EXPAND_ROWS):
        loads[group].wait()
        kept = min(rows, owned - start)

        for index, lanes in enumerate(tiles):
            if group == 0:
                basis_loads[index].wait()
            total = lax.dot_general(
                dirs[:, :, pl.ds(start, rows), :].reshape(8 * rows, rank), basis[lanes, :],
                (((1,), (1,)), ((), ())), preferred_element_type=F32,
            )
            for part_of in range(EXPAND_LANES // 128):
                column = index * (EXPAND_LANES // 128) + part_of
                for yl in range(2):
                    for x in range(4):
                        at = (yl * 4 + x) * rows
                        update[column, pl.ds(start * 8 + x * 2 + yl, kept, stride=8), :] = total[
                            at : at + kept, part_of * 128 : (part_of + 1) * 128
                        ]
        for column in range(depth // 128):
            place = pl.ds(start * 8, kept * 8)
            store = pltpu.make_async_copy(
                update.at[column, place], update_out.at[place, pl.ds(column * 128, 128)], store_sem.at[group, column]
            )
            store.start()
            stores.append(store)
        if group == 0:
            for copy_in, copy_out in zip(moments_in, moments_out):
                copy_in.wait()
                copy_out.start()
    for store in stores + moments_out:
        store.wait()


def expand(dirs, projector, first, second, owned):
    depth, rank = projector.shape[1:]
    in_hbm = pl.BlockSpec(memory_space=pl.ANY)
    moment = jax.ShapeDtypeStruct(first.shape, F32)
    return pl.pallas_call(
        expand_kernel,
        out_shape=(jax.ShapeDtypeStruct((owned * 8, depth), F32), moment, moment),
        in_specs=[in_hbm] * 4,
        out_specs=(in_hbm,) * 3,
        scratch_shapes=[
            pltpu.VMEM(dirs.shape, BF16),
            pltpu.VMEM((depth, rank), BF16),
            pltpu.VMEM((depth // 128, owned * 8, 128), F32),
            pltpu.VMEM(first.shape, F32),
            pltpu.VMEM(first.shape, F32),
            pltpu.SemaphoreType.DMA((len(EXPAND_ROWS),)),
            pltpu.SemaphoreType.DMA((depth // EXPAND_LANES,)),
            pltpu.SemaphoreType.DMA((len(EXPAND_ROWS), depth // 128)),
            pltpu.SemaphoreType.DMA((4,)),
        ],
        compiler_params=pltpu.CompilerParams(vmem_limit_bytes=60 << 20),
        name="expand",
    )(dirs, projector, first, second)


def local(activations, out_grads, projector, first_moment, second_moment):
    owned, rank = first_moment.shape[1:]
    flat = (owned * (rank // 128), 128)
    dirs, first, second = exchange(
        activations, jnp.swapaxes(out_grads, 1, 2), projector, first_moment.reshape(flat), second_moment.reshape(flat),
        owned,
    )
    update, first, second = expand(dirs, projector, first, second, owned)
    update = update.reshape(owned, 8, -1).transpose(1, 0, 2)[None]
    return update, first.reshape(first_moment.shape), second.reshape(second_moment.shape)


def solution(mesh):
    in_specs = (
        P(None, "dp", "fsdp"),
        P(None, "dp", "fsdp"),
        P(None, "fsdp", None),
        P(None, ("fsdp", "dp"), None),
        P(None, ("fsdp", "dp"), None),
    )
    out_specs = (
        P(None, None, "dp", "fsdp"),
        P(None, ("fsdp", "dp"), None),
        P(None, ("fsdp", "dp"), None),
    )
    return jax.shard_map(local, mesh=mesh, in_specs=in_specs, out_specs=out_specs, check_vma=False)
```

```python
import functools

import jax
import jax.numpy as jnp
from jax import lax
from jax.experimental import pallas as pl
from jax.experimental.pallas import tpu as pltpu
from jax.sharding import PartitionSpec as P

MESH = pl.DeviceIdType.MESH
F32, BF16 = jnp.float32, jnp.bfloat16

beta_first = 0.9
beta_second = 0.999
adam_count = 100.0
epsilon = 1e-08

CHUNKS = 8
RS_X_FIRST = (True, False, True, False, True, False, True, False)
AG_X_FIRST = (True, False, True, False, True, False, True, False)
DIR_X_FIRST = (True, False, True, False, True, False, True, False)
ORDER = (
    2, 3, 7, 0, 3, 6, 2, 1, 2, 3, 0, 7, 6, 3, 2, 1, 6, 0, 7, 5,
    2, 3, 6, 7, 4, 0, 2, 5, 3, 1, 7, 6, 4, 1, 2, 5, 7, 0, 3, 4,
    6, 1, 7, 5, 4, 2, 0, 6, 1, 7, 3, 2, 4, 5, 6, 3, 0, 7, 4, 1,
    2, 5, 6, 4, 3, 0, 1, 6, 7, 5, 0, 4, 1, 5, 4, 0, 1, 5, 4, 5,
)


def adam_direction(grad_low, first, second):
    first_next = beta_first * first + (1.0 - beta_first) * grad_low
    second_next = beta_second * second + (1.0 - beta_second) * grad_low * grad_low
    bias_first = 1.0 - beta_first**adam_count
    bias_second = 1.0 - beta_second**adam_count
    direction = first_next / bias_first / (jnp.sqrt(second_next / bias_second) + epsilon)
    return (first_next, second_next, direction.astype(BF16))


def wide(ref, *index):
    return ref[index].astype(F32)


def exchange_kernel(
    act_hbm, grads_hbm, basis_hbm, first_hbm, second_hbm,
    dirs_hbm, first_out, second_out,
    act, basis, grads_t, first, second, product,
    part, rs_a, rs_s, rs_b, projected,
    terms, core_in, z_out, z_in, y_out, y_in, dirs,
    load_sem, store_sem, send_sem, recv_sem,
):
    dp, fs = lax.axis_index("dp"), lax.axis_index("fsdp")
    yh, z, core = dp // 8, (dp // 2) % 4, dp % 2
    x, yl = fs // 2, fs % 2
    chunk = basis.shape[1] // CHUNKS
    row_tiles = basis.shape[1] // 128
    flat = pl.ds(0, first_hbm.shape[0])
    owned = first_hbm.shape[0] // row_tiles
    padded = dirs.shape[3]
    tokens = part.shape[3]
    features = act.shape[0]

    to_x = [None] + [(x + d) % 4 for d in (1, 2, 3)]
    to_z = [None] + [(z + d) % 4 for d in (1, 2, 3)]
    x_peers = [None] + [(dp, to_x[d] * 2 + yl) for d in (1, 2, 3)]
    z_peers = [None] + [(yh * 8 + to_z[d] * 2 + core, fs) for d in (1, 2, 3)]
    y_near = (dp, x * 2 + 1 - yl)
    y_far = ((1 - yh) * 8 + z * 2 + core, fs)
    sibling = (yh * 8 + z * 2 + 1 - core, fs)

    half = features // 2
    pair = 2 * chunk
    act_loads = [
        pltpu.make_async_copy(act_hbm.at[0, pl.ds(i * half, half)], act.at[pl.ds(i * half, half)], load_sem.at[i])
        for i in range(2)
    ]
    basis_loads = [
        pltpu.make_async_copy(
            basis_hbm.at[0, :, pl.ds(i * pair, pair)], basis.at[:, pl.ds(i * pair, pair)], load_sem.at[2 + i]
        )
        for i in range(CHUNKS // 2)
    ]
    grads_load = pltpu.make_async_copy(grads_hbm.at[0], grads_t, load_sem.at[2 + CHUNKS // 2])
    moment_loads = [
        pltpu.make_async_copy(first_hbm, first.at[flat], load_sem.at[3 + CHUNKS // 2]),
        pltpu.make_async_copy(second_hbm, second.at[flat], load_sem.at[4 + CHUNKS // 2]),
    ]
    pairs = list(dict.fromkeys(c // 2 for c in ORDER))
    basis_loads[pairs[0]].start()
    for load in act_loads + [basis_loads[i] for i in pairs[1:]] + [grads_load] + moment_loads:
        load.start()

    barrier = pltpu.get_barrier_semaphore()
    peers = x_peers[1:] + z_peers[1:] + [y_near, y_far, sibling]
    for peer in peers:
        pl.semaphore_signal(barrier, inc=1, device_id=peer, device_id_type=MESH)

    sent = [[] for _ in range(CHUNKS)]

    def remote(source, target, c, slot, peer):
        return pltpu.make_async_remote_copy(
            src_ref=source, dst_ref=target, send_sem=send_sem.at[c, slot], recv_sem=recv_sem.at[c, slot],
            device_id=peer, device_id_type=MESH,
        )

    def send(source, target, c, slot, peer):
        copy = remote(source, target, c, slot, peer)
        copy.start()
        sent[c].append(copy)

    def arrived(target, c, slot, peer):
        remote(target, target, c, slot, peer).wait_recv()


    def project(c):
        basis_loads[c // 2].wait()
        for index in range(2):
            if "act" not in waited:
                act_loads[index].wait()
            value = jnp.dot(
                act[index * half : (index + 1) * half, :], basis[:, c * chunk : (c + 2) * chunk],
                preferred_element_type=F32,
            ).astype(BF16)
            for which in range(2):
                part[c + which, index] = value[:, which * chunk : (which + 1) * chunk].reshape(4, tokens, chunk)
        waited.add("act")

    def reduce_first(c):
        if RS_X_FIRST[c]:
            for d in (2, 1, 3):
                send(part.at[c, :, to_x[d]], rs_a.at[c, pl.ds((d - 1) * 2, 2)], c, d - 1, x_peers[d])
        else:
            send(part.at[c, 1 - yl], rs_a.at[c, pl.ds(0, 4)], c, 3, y_near)

    def reduce_second(c):
        if RS_X_FIRST[c]:
            for d in (1, 3, 2):
                arrived(rs_a.at[c, pl.ds((d - 1) * 2, 2)], c, d - 1, x_peers[d])
            other = 1 - yl

            total = wide(part, c, other, x)
            for d in range(3):
                total += wide(rs_a, c, 2 * d + other)
            rs_s[c, 0] = total.astype(BF16)
            send(rs_s.at[c, 0], rs_b.at[c, 0], c, 3, y_near)
        else:
            arrived(rs_a.at[c, pl.ds(0, 4)], c, 3, y_near)
            for d in (2, 1, 3):
                to = to_x[d]
                rs_s[c, d - 1] = (wide(part, c, yl, to) + wide(rs_a, c, to)).astype(BF16)
                send(rs_s.at[c, d - 1], rs_b.at[c, d - 1], c, d - 1, x_peers[d])

    def reduce_last(c):
        if RS_X_FIRST[c]:
            arrived(rs_b.at[c, 0], c, 3, y_near)
            total = wide(part, c, yl, x) + wide(rs_b, c, 0)
            for d in range(3):
                total += wide(rs_a, c, 2 * d + yl)
        else:
            for d in (1, 3, 2):
                arrived(rs_b.at[c, d - 1], c, d - 1, x_peers[d])
            total = wide(part, c, yl, x) + wide(rs_a, c, x)
            for d in range(3):
                total += wide(rs_b, c, d)
        projected[c, yl, x] = total.astype(BF16)

    def gather_first(buffer, target, c, slot, x_first):
        mine, there = buffer.at[c, yl, x], target.at[yl, x]
        send(mine, there if x_first else mine, c, slot + 3, y_near)
        for d in (2, 1, 3):
            send(mine, mine if x_first else there, c, slot + d - 1, x_peers[d])

    def gather_second(buffer, target, c, slot, x_first):
        if x_first:
            for d in (1, 3, 2):
                block = (yl, to_x[4 - d])
                arrived(buffer.at[(c,) + block], c, slot + d - 1, x_peers[d])
                send(buffer.at[(c,) + block], target.at[block], c, slot + 3 + d, y_near)
        else:
            block = (1 - yl, x)
            arrived(buffer.at[(c,) + block], c, slot + 3, y_near)
            for d in (2, 1, 3):
                send(buffer.at[(c,) + block], target.at[block], c, slot + 3 + d, x_peers[d])

    def gather_last(target, c, slot, x_first):
        if x_first:
            arrived(target.at[1 - yl, x], c, slot + 3, y_near)
            for d in (1, 3, 2):
                arrived(target.at[1 - yl, to_x[4 - d]], c, slot + 3 + d, y_near)
        else:
            for d in (1, 3, 2):
                arrived(target.at[yl, to_x[4 - d]], c, slot + d - 1, x_peers[d])
            for d in (1, 3, 2):
                arrived(target.at[1 - yl, to_x[4 - d]], c, slot + 3 + d, x_peers[d])

    def gradient(first_c):
        rows_all = grads_t.shape[0]
        tile = rows_all // 4

        def one(index, carry):
            rows = pl.ds(pl.multiple_of(index * tile, tile), tile)
            right = jnp.concatenate([projected[first_c + k].reshape(features, chunk) for k in range(2)], axis=1)
            product[rows, :] = jnp.dot(grads_t[rows, :], right, preferred_element_type=F32)
            return carry

        lax.fori_loop(0, 4, one, 0)

        def blocks_of(which):
            shift = which * owned % 8

            def two(block, carry):
                start = pl.multiple_of(block * (2 * owned) + which * owned - shift, 8)
                value = product[pl.ds(start, padded + 8), :]
                value = value[shift : shift + padded].astype(BF16)
                for k in range(2):
                    terms[first_c + k, which, block // 4, block % 4] = value[:, k * chunk : (k + 1) * chunk]
                return carry

            lax.fori_loop(0, 8, two, 0)

        lax.cond(core == 0, lambda: blocks_of(1), lambda: blocks_of(0))
        for c in (first_c, first_c + 1):
            send(terms.at[c, 1 - core], core_in.at[c], c, 11, sibling)
        lax.cond(core == 0, lambda: blocks_of(0), lambda: blocks_of(1))

    def core_sum(c):
        arrived(core_in.at[c], c, 11, sibling)
        for h, slot in ((1 - yh, 11), (yh, 14)):
            for d in (2, 1, 3):
                to = to_z[d]
                z_out[c, d - 1, h] = (wide(terms, c, core, h, to) + wide(core_in, c, h, to)).astype(BF16)
                send(z_out.at[c, d - 1, h], z_in.at[c, d - 1, h], c, slot + d, z_peers[d])

    def z_arrived(c, h, slot):
        for d in (1, 3, 2):
            arrived(z_in.at[c, d - 1, h], c, slot + d, z_peers[d])

    def z_sum(c, h):
        total = wide(terms, c, core, h, z) + wide(core_in, c, h, z)
        for d in range(3):
            total += wide(z_in, c, d, h)
        return total

    def z_stage(c):
        z_arrived(c, 1 - yh, 11)
        y_out[c] = z_sum(c, 1 - yh).astype(BF16)
        send(y_out.at[c], y_in.at[c], c, 18, y_far)

    def adam(c):
        if "moments" not in waited:
            for load in moment_loads:
                load.wait()
            waited.add("moments")
        z_arrived(c, yh, 14)
        arrived(y_in.at[c], c, 18, y_far)

        low = (z_sum(c, yh) + wide(y_in, c))[:owned]
        for part_of in range(chunk // 128):
            lanes = slice(part_of * 128, (part_of + 1) * 128)
            here = pl.ds(c * (chunk // 128) + part_of, owned, stride=row_tiles)
            first_next, second_next, direction = adam_direction(low[:, lanes], first[here, :], second[here, :])
            first[here, :] = first_next
            second[here, :] = second_next
            dirs[c, yl, x, :owned, lanes] = direction

    def dirs_out(c):
        return dirs_hbm.at[:, :, :, pl.ds(c * chunk, chunk)]

    def out_copies(c):
        if DIR_X_FIRST[c]:
            return pltpu.make_async_copy(dirs.at[c, yl], dirs_out(c).at[yl], store_sem.at[c, 0])
        return pltpu.make_async_copy(dirs.at[c, :, x], dirs_out(c).at[:, x], store_sem.at[c, 0])

    barrier_done, projected_pairs, waited, gathered = [], set(), set(), set()

    def stage(s, c):
        if s == 0:
            if c // 2 not in projected_pairs:
                project(c // 2 * 2)
                projected_pairs.add(c // 2)
            if not barrier_done:
                pl.semaphore_wait(barrier, len(peers))
                barrier_done.append(True)
            reduce_first(c)
        elif s == 1:
            reduce_second(c)
        elif s == 2:
            reduce_last(c)
            gather_first(projected, projected.at[c], c, 4, AG_X_FIRST[c])
        elif s == 3:
            gather_second(projected, projected.at[c], c, 4, AG_X_FIRST[c])
        elif s == 4:
            gather_last(projected.at[c], c, 4, AG_X_FIRST[c])
            if "grads" not in waited:
                grads_load.wait()
                waited.add("grads")
            if c ^ 1 in gathered:
                gradient(c // 2 * 2)
            gathered.add(c)
        elif s == 5:
            done = sent[c][:-1]
            core_sum(c)
            for copy in done:
                copy.wait_send()
            del sent[c][: len(done)]
        elif s == 6:
            z_stage(c)
        elif s == 7:
            adam(c)
            gather_first(dirs, dirs_out(c), c, 19, DIR_X_FIRST[c])
        elif s == 8:
            done = sent[c][:8]
            gather_second(dirs, dirs_out(c), c, 19, DIR_X_FIRST[c])
            out_copies(c).start()
            for copy in done:
                copy.wait_send()
            del sent[c][: len(done)]
        else:
            gather_last(dirs_out(c), c, 19, DIR_X_FIRST[c])
            for copy in sent[c]:
                copy.wait_send()
            out_copies(c).wait()

    order, turns = [], [0] * CHUNKS
    for c in ORDER:
        order.append((None, c, turns[c]))
        turns[c] += 1
    moments = [
        pltpu.make_async_copy(first.at[flat], first_out, store_sem.at[CHUNKS, 0]),
        pltpu.make_async_copy(second.at[flat], second_out, store_sem.at[CHUNKS + 1, 0]),
    ]
    last_adam = [c for _, c, s in order if s == 7][-1]
    for _, c, s in order:
        stage(s, c)
        if s == 7 and c == last_adam:
            for copy in moments:
                copy.start()
    for copy in moments:
        copy.wait()


def exchange(activations, grads_t, projector, first, second, owned):
    features = activations.shape[1]
    width = grads_t.shape[1]
    depth, rank = projector.shape[1:]
    padded = -(-owned // 16) * 16
    chunk = rank // CHUNKS
    tokens = features // 8
    in_hbm = pl.BlockSpec(memory_space=pl.ANY)
    C = CHUNKS
    scratch = [
        pltpu.VMEM((features, depth), BF16),
        pltpu.VMEM((depth, rank), BF16),
        pltpu.VMEM((width, features), BF16),
        pltpu.VMEM((padded * (rank // 128), 128), F32),
        pltpu.VMEM((padded * (rank // 128), 128), F32),
        pltpu.VMEM((width + 16, 2 * chunk), F32),
        pltpu.VMEM((C, 2, 4, tokens, chunk), BF16),
        pltpu.VMEM((C, 6, tokens, chunk), BF16),
        pltpu.VMEM((C, 3, tokens, chunk), BF16),
        pltpu.VMEM((C, 3, tokens, chunk), BF16),
        pltpu.VMEM((C, 2, 4, tokens, chunk), BF16),
        pltpu.VMEM((C, 2, 2, 4, padded, chunk), BF16),
        pltpu.VMEM((C, 2, 4, padded, chunk), BF16),
        pltpu.VMEM((C, 3, 2, padded, chunk), BF16),
        pltpu.VMEM((C, 3, 2, padded, chunk), BF16),
        pltpu.VMEM((C, padded, chunk), BF16),
        pltpu.VMEM((C, padded, chunk), BF16),
        pltpu.VMEM((C, 2, 4, padded, chunk), BF16),
        pltpu.SemaphoreType.DMA((5 + C // 2,)),
        pltpu.SemaphoreType.DMA((C + 2, 2)),
        pltpu.SemaphoreType.DMA((C, 26)),
        pltpu.SemaphoreType.DMA((C, 26)),
    ]
    return pl.pallas_call(
        exchange_kernel,
        out_shape=(
            jax.ShapeDtypeStruct((2, 4, padded, rank), BF16),
            jax.ShapeDtypeStruct(first.shape, F32),
            jax.ShapeDtypeStruct(first.shape, F32),
        ),
        in_specs=[in_hbm] * 5,
        out_specs=(in_hbm,) * 3,
        scratch_shapes=scratch,
        compiler_params=pltpu.CompilerParams(
            collective_id=0, has_side_effects=True, vmem_limit_bytes=60 << 20
        ),
        name="exchange",
    )(activations, grads_t, projector, first, second)


EXPAND_ROWS = ((0, 64), (64, 80), (144, 32))
EXPAND_LANES = 512


def expand_kernel(
    dirs_hbm, basis_hbm, first_in, second_in, update_out, first_out, second_out,
    dirs, basis, update, first, second, load_sem, basis_sem, store_sem, sem,
):
    rank = dirs.shape[3]
    depth = basis.shape[0]
    owned = update_out.shape[0] // 8
    tiles = [pl.ds(lane, EXPAND_LANES) for lane in range(0, depth, EXPAND_LANES)]
    basis_loads = [
        pltpu.make_async_copy(basis_hbm.at[0, lanes], basis.at[lanes], basis_sem.at[index])
        for index, lanes in enumerate(tiles)
    ]
    loads = [
        pltpu.make_async_copy(dirs_hbm.at[:, :, pl.ds(*rows)], dirs.at[:, :, pl.ds(*rows)], load_sem.at[group])
        for group, rows in enumerate(EXPAND_ROWS)
    ]
    basis_loads[0].start()
    for load in loads[:1] + basis_loads[1:] + loads[1:]:
        load.start()
    moments_in = [
        pltpu.make_async_copy(first_in, first, sem.at[0]),
        pltpu.make_async_copy(second_in, second, sem.at[1]),
    ]
    moments_out = [
        pltpu.make_async_copy(first, first_out, sem.at[2]),
        pltpu.make_async_copy(second, second_out, sem.at[3]),
    ]
    for copy in moments_in:
        copy.start()
    stores = []
    for group, (start, rows) in enumerate(EXPAND_ROWS):
        loads[group].wait()
        kept = min(rows, owned - start)

        for index, lanes in enumerate(tiles):
            if group == 0:
                basis_loads[index].wait()
            total = lax.dot_general(
                dirs[:, :, pl.ds(start, rows), :].reshape(8 * rows, rank), basis[lanes, :],
                (((1,), (1,)), ((), ())), preferred_element_type=F32,
            )
            for part_of in range(EXPAND_LANES // 128):
                column = index * (EXPAND_LANES // 128) + part_of
                for yl in range(2):
                    for x in range(4):
                        at = (yl * 4 + x) * rows
                        update[column, pl.ds(start * 8 + x * 2 + yl, kept, stride=8), :] = total[
                            at : at + kept, part_of * 128 : (part_of + 1) * 128
                        ]
        for column in range(depth // 128):
            place = pl.ds(start * 8, kept * 8)
            store = pltpu.make_async_copy(
                update.at[column, place], update_out.at[place, pl.ds(column * 128, 128)], store_sem.at[group, column]
            )
            store.start()
            stores.append(store)
        if group == 0:
            for copy_in, copy_out in zip(moments_in, moments_out):
                copy_in.wait()
                copy_out.start()
    for store in stores + moments_out:
        store.wait()


def expand(dirs, projector, first, second, owned):
    depth, rank = projector.shape[1:]
    in_hbm = pl.BlockSpec(memory_space=pl.ANY)
    moment = jax.ShapeDtypeStruct(first.shape, F32)
    return pl.pallas_call(
        expand_kernel,
        out_shape=(jax.ShapeDtypeStruct((owned * 8, depth), F32), moment, moment),
        in_specs=[in_hbm] * 4,
        out_specs=(in_hbm,) * 3,
        scratch_shapes=[
            pltpu.VMEM(dirs.shape, BF16),
            pltpu.VMEM((depth, rank), BF16),
            pltpu.VMEM((depth // 128, dirs.shape[2] * 8, 128), F32),
            pltpu.VMEM(first.shape, F32),
            pltpu.VMEM(first.shape, F32),
            pltpu.SemaphoreType.DMA((len(EXPAND_ROWS),)),
            pltpu.SemaphoreType.DMA((depth // EXPAND_LANES,)),
            pltpu.SemaphoreType.DMA((len(EXPAND_ROWS), depth // 128)),
            pltpu.SemaphoreType.DMA((4,)),
        ],
        compiler_params=pltpu.CompilerParams(vmem_limit_bytes=60 << 20),
        name="expand",
    )(dirs, projector, first, second)


def local(activations, out_grads, projector, first_moment, second_moment):
    owned, rank = first_moment.shape[1:]
    flat = (owned * (rank // 128), 128)
    dirs, first, second = exchange(
        activations, jnp.swapaxes(out_grads, 1, 2), projector, first_moment.reshape(flat), second_moment.reshape(flat),
        owned,
    )
    update, first, second = expand(dirs, projector, first, second, owned)
    update = update.reshape(owned, 8, -1).transpose(1, 0, 2)[None]
    return update, first.reshape(first_moment.shape), second.reshape(second_moment.shape)


def solution(mesh):
    in_specs = (
        P(None, "dp", "fsdp"),
        P(None, "dp", "fsdp"),
        P(None, "fsdp", None),
        P(None, ("fsdp", "dp"), None),
        P(None, ("fsdp", "dp"), None),
    )
    out_specs = (
        P(None, None, "dp", "fsdp"),
        P(None, ("fsdp", "dp"), None),
        P(None, ("fsdp", "dp"), None),
    )
    return jax.shard_map(local, mesh=mesh, in_specs=in_specs, out_specs=out_specs, check_vma=False)
```
